32 devices in a mesh: gx: 8 (over z, y), gy: 4 (over x, core).
Axes of the slice: x: 2, y: 2, z: 4, core: 2. Of those that a mesh axis runs over, the one named last changes fastest.
Arguments:
- state: float32 [2048, 1, 8, 2048], P('gx', None, None, 'gy'), may hold values from -1 to 1, as said below
- mobility: float32 [2048, 1, 2048], P('gx', None, 'gy'), may hold values from 0.22 to 4.5, as said below
Outputs:
- new_state: float32 [2048, 1, 8, 2048], P('gx', None, None, 'gy')
The draws below stay inside these ranges and needn't reach their ends.
Inputs may be any that keep to these rules, and one draw needn't show every extreme that they name: `state`: each order parameter's value at a cell. Each cell's mobility.
All inputs are finite; a program needn't handle non-finite values.
Results may differ from the reference program's by a relative error of at most 0.0054.
Values sent between devices are 32-bit elements; how exact they have to be, the bound alone decides.
No kernel may reach another device: no remote copies, remote signals or barrier semaphores. Data moves between devices by JAX's collectives and lax.ppermute only.
A program may use at most 128 MiB of HBM per device.

```python
import math
import jax
import jax.numpy as jnp
from jax import lax

NX = 2048
NY = 2048
K = 8
PLANES = 1


def draw_state(key, part):
    key = jax.random.fold_in(key, 11)
    shape = (NX, PLANES, K, NY)
    base = jax.random.uniform(key, shape, jnp.float32, -1.0, 1.0)
    texture = jnp.roll(base, 1, 0) + jnp.roll(base, -1, 0) + jnp.roll(base, 1, 3) + jnp.roll(base, -1, 3) - 4.0 * base
    return 0.079 * texture


def draw_mobility(key, part):
    key = jax.random.fold_in(key, 23)
    shape = (NX, PLANES, NY)
    row_place = jnp.arange(NX, dtype=jnp.float32) / NX
    col_place = jnp.arange(NY, dtype=jnp.float32) / NY
    base = jnp.exp(jax.random.uniform(key, shape, jnp.float32, math.log(0.5), math.log(2.0)))
    ramp = 0.5 * math.log(3.0)
    envelope = jnp.exp(ramp * (row_place[:, None, None] + col_place[None, None, :] - 1.0))
    return base * envelope


def setup_inputs(seed: int = 0) -> dict:
    key_of = jax.random.split(jax.random.key(seed), 3)
    state = draw_state(jax.random.fold_in(key_of[2], 71), 0)
    mobility = draw_mobility(jax.random.fold_in(key_of[2], 71), 0)
    return {"state": state, "mobility": mobility}


linear_coef = 1.0
cubic_coef = 1.0
cross_coef = 1.5
gradient_coef = 200.0
time_step = 200.0

def hartley(size):
    places = jnp.arange(size, dtype=jnp.int32)
    phase = places[:, None] * places[None, :] % size
    angle = phase.astype(jnp.float32) * (2.0 * math.pi / size)
    return jnp.cos(angle) + jnp.sin(angle)

def symbol(freq_x, freq_y, size_x, size_y):
    sine_x = jnp.sin(freq_x * (math.pi / size_x))
    sine_y = jnp.sin(freq_y * (math.pi / size_y))
    return 1.0 + time_step * gradient_coef * (4.0 * sine_x * sine_x + 4.0 * sine_y * sine_y)

def laplace(field):
    inplane = jnp.roll(field, 1, 0) + jnp.roll(field, -1, 0) + jnp.roll(field, 1, 3) + jnp.roll(field, -1, 3) - 4.0 * field
    lower = jnp.concatenate([field[:, :1], field[:, :-1]], axis=1)
    upper = jnp.concatenate([field[:, 1:], field[:, -1:]], axis=1)
    return inplane + lower + upper - 2.0 * field

def precondition(vector, table_x, table_y):
    highest = lax.Precision.HIGHEST
    along_x = jnp.tensordot(table_x, vector, axes=(1, 0), precision=highest)
    spectrum = jnp.tensordot(along_x, table_y, axes=(3, 0), precision=highest)
    freq_x = jnp.arange(NX, dtype=jnp.float32)[:, None, None, None]
    freq_y = jnp.arange(NY, dtype=jnp.float32)[None, None, None, :]
    scaled = spectrum / (symbol(freq_x, freq_y, NX, NY) * float(NX * NY))
    back_y = jnp.tensordot(scaled, table_y, axes=(3, 1), precision=highest)
    return jnp.tensordot(table_x, back_y, axes=(1, 0), precision=highest)

def least_squares(beta, top_left, below_first, top_right, middle_right, bottom_right):
    first_radius = jnp.sqrt(top_left * top_left + below_first * below_first)
    first_cosine = top_left / first_radius
    first_sine = below_first / first_radius
    upper_right = first_cosine * top_right + first_sine * middle_right
    lower_right = -first_sine * top_right + first_cosine * middle_right
    upper_target = first_cosine * beta
    lower_target = -first_sine * beta
    second_radius = jnp.sqrt(lower_right * lower_right + bottom_right * bottom_right)
    second_cosine = lower_right / second_radius
    second_coef = second_cosine * lower_target / second_radius
    first_coef = (upper_target - upper_right * second_coef) / first_radius
    return (first_coef, second_coef)

def reference(state, mobility):
    table_x = hartley(NX)
    table_y = hartley(NY)
    squares = state * state
    total = lax.optimization_barrier(jnp.sum(squares, axis=2, keepdims=True))
    reaction = -linear_coef + 3.0 * cubic_coef * squares + 2.0 * cross_coef * (total - squares)
    rate = time_step * mobility[:, :, None, :]

    def jacobian(vector):
        coupled = lax.optimization_barrier(jnp.sum(state * vector, axis=2, keepdims=True))
        return vector + rate * (reaction * vector + 4.0 * cross_coef * state * (coupled - state * vector) - gradient_coef * laplace(vector))
    force = rate * (-linear_coef * state + cubic_coef * squares * state + 2.0 * cross_coef * state * (total - squares) - gradient_coef * laplace(state))
    start = -force
    beta = jnp.sqrt(jnp.sum(start * start))
    first = start / beta
    search_one = precondition(first, table_x, table_y)
    image = jacobian(search_one)
    top_left = jnp.sum(first * image)
    image = image - top_left * first
    below_first = jnp.sqrt(jnp.sum(image * image))
    second = image / below_first
    search_two = precondition(second, table_x, table_y)
    image = jacobian(search_two)
    top_right = jnp.sum(first * image)
    middle_right = jnp.sum(second * image)
    image = image - top_right * first
    image = image - middle_right * second
    bottom_right = jnp.sqrt(jnp.sum(image * image))
    first_coef, second_coef = least_squares(beta, top_left, below_first, top_right, middle_right, bottom_right)
    update = first_coef * search_one + second_coef * search_two
    return state + update
```

```python
import functools
import math

import jax
import jax.numpy as jnp
import numpy as np
from jax import lax
from jax.experimental import pallas as pl
from jax.experimental.pallas import tpu as pltpu
from jax.sharding import PartitionSpec as P

linear_coef = 1.0
cubic_coef = 1.0
cross_coef = 1.5
gradient_coef = 200.0
time_step = 200.0
stiffness = time_step * gradient_coef

F32 = jnp.float32
BF16 = jnp.bfloat16
VMEM_LIMIT = 56 * 1024 * 1024


def cosine_table(size):
    modes = np.arange(size)[:, None]
    cells = np.arange(size)[None, :]
    table = np.sqrt(2.0 / size) * np.cos(np.pi * modes * (cells + 0.5) / size)
    table[0] = np.sqrt(1.0 / size)
    values = 4.0 * np.sin(np.pi * np.arange(size) / (2 * size)) ** 2
    order = np.concatenate([np.arange(0, size, 2), np.arange(1, size, 2)])
    return table[order], values[order]


def split_const(table):
    high = table.astype(np.float32).astype(jnp.bfloat16)
    low = (table - high.astype(np.float64)).astype(np.float32).astype(jnp.bfloat16)
    return high, low


def right_const(table):
    high, low = split_const(table)
    return np.concatenate([high, low, high], axis=0)


def left_const(table):
    high, low = split_const(table)
    return np.concatenate([high, low, high], axis=1)


def make_tables(lx, ly, gx, gy):
    cos_x, value_x = cosine_table(lx)
    cos_y, value_y = cosine_table(ly)
    edge_x, edge_y = cos_x[:, 0], cos_y[:, 0]
    inverse = 1.0 / (1.0 + stiffness * (value_x[:, None] + value_y[None, :]))
    cross = edge_x[:, None] * edge_y[None, :] * inverse
    sign_x = np.where(np.arange(lx) < lx // 2, 1.0, -1.0)
    sign_y = np.where(np.arange(ly) < ly // 2, 1.0, -1.0)
    own = (edge_x[:, None] ** 2 * inverse).sum(0)
    other = (sign_x[:, None] * edge_x[:, None] ** 2 * inverse).sum(0)
    wave = np.arange(gx)
    eigen = 1.0 / stiffness + 2.0 * own[None] - 2.0 * other[None] * np.cos(2 * np.pi * wave / gx)[:, None]
    gap_x = np.stack(
        [(np.cos(2 * np.pi * wave * d / gx)[:, None] / eigen).mean(0) for d in range(gx // 2 + 1)]
    )
    total = lx * gx
    half = gx // 2 + 1
    rows = -(-half * gy // 8) * 8
    freq = gx * np.arange(lx)[None, :] + np.arange(half)[:, None]
    symbol = 1.0 + stiffness * (4.0 * np.sin(np.pi * freq / total) ** 2)[:, :, None] + stiffness * value_y
    own = (edge_y**2 / symbol).sum(-1)
    other = (sign_y * edge_y**2 / symbol).sum(-1)
    wave = np.arange(gy)
    eigen = 1.0 / stiffness + 2.0 * own[None] - 2.0 * other[None] * np.cos(2 * np.pi * wave / gy)[:, None, None]
    gap_y = np.zeros((gy // 2 + 1, 2 * rows, lx))
    for d in range(gy // 2 + 1):
        coef = (np.cos(2 * np.pi * wave * d / gy)[:, None, None] / eigen).mean(0)
        coef = np.repeat(coef, gy, axis=0)
        gap_y[d, : half * gy] = coef
        gap_y[d, rows : rows + half * gy] = coef
    cells = np.arange(lx)
    angle = 2 * np.pi * np.outer(cells, cells) / lx
    fourier = np.concatenate([np.cos(angle), np.sin(angle)], axis=1)
    twist = np.zeros((2, rows, lx))
    gather = np.zeros((2 * rows, gx * gy))
    scatter = np.zeros((gx * gy, 2 * rows))
    for q in range(half):
        theta = 2 * np.pi * q * cells / total
        weight = (1.0 if q in (0, gx // 2) else 2.0) / total
        for j in range(gy):
            twist[0, q * gy + j] = np.cos(theta)
            twist[1, q * gy + j] = np.sin(theta)
            for i in range(gx):
                phase = 2 * np.pi * q * i / gx
                gather[q * gy + j, i * gy + j] = np.cos(phase)
                gather[rows + q * gy + j, i * gy + j] = -np.sin(phase)
                scatter[i * gy + j, q * gy + j] = weight * np.cos(phase)
                scatter[i * gy + j, rows + q * gy + j] = -weight * np.sin(phase)
    single = lambda a: np.ascontiguousarray(a, dtype=np.float32)
    zero_x, zero_y = np.zeros(lx // 2), np.zeros(ly // 2)
    ends_x = np.zeros((8, lx))
    ends_x[0], ends_x[1] = (
        np.concatenate([edge_x[: lx // 2], zero_x]),
        np.concatenate([zero_x, edge_x[lx // 2 :]]),
    )
    ends_y = np.zeros((8, ly))
    ends_y[2], ends_y[3] = (
        np.concatenate([edge_y[: ly // 2], zero_y]),
        np.concatenate([zero_y, edge_y[ly // 2 :]]),
    )
    main = dict(
        fwd_y=right_const(cos_y.T),
        fwd_x=left_const(cos_x),
        inv_y=right_const(cos_y),
        inv_x=left_const(cos_x.T),
        inverse=single(inverse),
        edge_x=single(edge_x[:, None]),
        edge_y=single(edge_y[None, :]),
        ends_x=single(ends_x),
        ends_y=single(ends_y),
    )
    face = dict(
        cross=single(cross),
        cross_t=single(cross.T),
        cos_x=single(cos_x),
        cos_xt=single(cos_x.T),
        gap_x=single(gap_x),
        gap_y=single(gap_y),
        fourier=single(fourier),
        twist=single(twist),
        gather=single(gather),
        scatter=single(scatter),
    )
    return main, face


def halves(x):
    high = x.astype(BF16)
    low = (x - high.astype(F32)).astype(BF16)
    return high, low


def times_right(x, const):
    high, low = halves(x)
    return jnp.dot(jnp.concatenate([high, high, low], axis=1), const[...], preferred_element_type=F32)


def times_left(const, x):
    high, low = halves(x)
    return jnp.dot(const[...], jnp.concatenate([high, high, low], axis=0), preferred_element_type=F32)


def thirds(x):
    high = x.astype(BF16).astype(F32)
    rest = x - high
    mid = rest.astype(BF16).astype(F32)
    return high, mid, rest - mid


def outer_sum(a, b):
    ah, am, al = thirds(a)
    bh, bm, bl = thirds(b)
    left = jnp.concatenate([ah, ah, am, am, ah, al], axis=0).astype(BF16)
    right = jnp.concatenate([bh, bm, bh, bm, bl, bh], axis=0).astype(BF16)
    return lax.dot_general(left, right, (((0,), (0,)), ((), ())), preferred_element_type=F32)


def transform_out(field, k, spec, pay, tabs, dest):
    lx, ly = field.shape[1:]
    hat = times_left(tabs["fwd_x"], times_right(field[k], tabs["fwd_y"]))
    spectrum = hat * tabs["inverse"][...]
    spec[k] = spectrum
    weighted = spectrum * tabs["edge_x"][...]
    top = [
        jnp.sum(weighted[: lx // 2], axis=0, keepdims=True),
        jnp.sum(weighted[lx // 2 :], axis=0, keepdims=True),
    ]
    weighted = spectrum * tabs["edge_y"][...]
    cols = [weighted[:, i * 128 : (i + 1) * 128] for i in range(ly // 128)]
    half = len(cols) // 2
    folded = jnp.concatenate([sum(cols[1:half], cols[0]), sum(cols[half + 1 :], cols[half])], axis=0)
    high, low = halves(folded)
    ones = jnp.ones((8, 256), BF16)
    side = lax.dot_general(
        ones, jnp.concatenate([high, low], axis=1), (((1,), (1,)), ((), ())), preferred_element_type=F32
    )[:1]
    line = jnp.concatenate([*top, side], axis=1)
    for d in dest(k):
        for j in range(line.shape[1] // 128):
            pay[d, j : j + 1, :] = line[:, j * 128 : (j + 1) * 128]


def transform_back(spec, k, corr, field, tabs):
    lx, ly = field.shape[1:]
    nx, ny = lx // 128, ly // 128
    piece = lambda start, count: jnp.concatenate(
        [corr[k, start + j : start + j + 1, :] for j in range(count)], axis=1
    )
    row = lax.broadcasted_iota(jnp.int32, (8, 1), 0)
    a = (
        tabs["ends_x"][...]
        + jnp.where(row == 2, piece(2 * ny, nx), 0.0)
        + jnp.where(row == 3, piece(2 * ny + nx, nx), 0.0)
    )
    b = (
        tabs["ends_y"][...]
        + jnp.where(row == 0, piece(0, ny), 0.0)
        + jnp.where(row == 1, piece(ny, ny), 0.0)
    )
    spectrum = spec[k] + tabs["inverse"][...] * outer_sum(a, b)
    return times_left(tabs["inv_x"], times_right(spectrum, tabs["inv_y"]))


def lane_sum(x):
    return jnp.sum(x, axis=0, keepdims=True)


def store_sums(pay, start, rows):
    for j, row in enumerate(rows):
        for d in range(pay.shape[0]):
            pay[d, start + j : start + j + 1, :] = row


MAIN = ("fwd_y", "fwd_x", "inv_y", "inv_x", "inverse", "edge_x", "edge_y", "ends_x", "ends_y")
FACE = (
    "cross",
    "cross_t",
    "cos_x",
    "cos_xt",
    "gap_x",
    "gap_y",
    "fourier",
    "twist",
    "gather",
    "scatter",
)


def destinations(k, kinds, gx, gy):
    return [k * gy + p + kinds * gy * copy for copy in range(gx // kinds) for p in range(gy)]


def start_kernel(gx, gy, nrow, *refs):
    state, mob_hbm, edge_lo, edge_hi, side = refs[:5]
    tabs = dict(zip(("fwd_y", "fwd_x", "inverse", "edge_x", "edge_y"), refs[5:10]))
    r0_out, spec_out, pay = refs[10:13]
    st, mob, field, spec, acc, sem, out_sem = refs[13:]
    kinds, lx, ly = field.shape
    copies = [
        pltpu.make_async_copy(state.at[:, 0, k, :], st.at[k, pl.ds(8, lx), :], sem.at[k]) for k in range(kinds)
    ]
    for copy in copies:
        copy.start()
    mob_copy = pltpu.make_async_copy(mob_hbm.at[:, 0, :], mob, sem.at[kinds])
    mob_copy.start()
    for k in range(kinds):
        st[k, 7:8, :] = edge_lo[0, 0, k : k + 1, :]
        st[k, lx + 8 : lx + 9, :] = edge_hi[0, 0, k : k + 1, :]
    acc[...] = jnp.zeros_like(acc)
    mob_copy.wait()
    for copy in copies:
        copy.wait()
    lane = lax.broadcasted_iota(jnp.int32, (8, ly), 1)

    @pl.loop(0, lx // 8)
    def _(i):
        row = pl.multiple_of(i * 8, 8)
        rate = time_step * mob[pl.ds(row, 8), :]
        tall = [st[k, pl.ds(row, 24), :] for k in range(kinds)]
        mids = [block[8:16] for block in tall]
        total = sum(m * m for m in mids)
        base = -linear_coef + 2.0 * cross_coef * total
        norm = jnp.zeros((8, ly), F32)
        for k in range(kinds):
            mid = mids[k]
            around = tall[k][7:15] + tall[k][9:17]
            beside = side[k, pl.ds(row, 8), :]
            left = jnp.where(lane == 0, beside[:, 0:1], pltpu.roll(mid, 1, 1))
            right = jnp.where(lane == ly - 1, beside[:, 1:2], pltpu.roll(mid, ly - 1, 1))
            lap = around + left + right - 4.0 * mid
            react = mid * (base + (cubic_coef - 2.0 * cross_coef) * (mid * mid))
            value = rate * (gradient_coef * lap - react)
            field[k, pl.ds(row, 8), :] = value
            norm = norm + value * value
        acc[...] += sum(norm[:, j * 128 : (j + 1) * 128] for j in range(ly // 128))

    out = pltpu.make_async_copy(field, r0_out, out_sem.at[0])
    out.start()

    @pl.loop(0, kinds)
    def _(k):
        transform_out(field, k, spec, pay, tabs, lambda k: destinations(k, kinds, gx, gy))

    spec_copy = pltpu.make_async_copy(spec, spec_out, out_sem.at[1])
    spec_copy.start()
    store_sums(pay, nrow, [lane_sum(acc[...])])
    out.wait()
    spec_copy.wait()


def load_all(sources, kinds, sem):
    copies = [pltpu.make_async_copy(s, d, sem.at[j]) for j, (s, d) in enumerate(sources)]
    for copy in copies:
        copy.start()
    return copies


def middle_kernel(gx, gy, nrow, *refs):
    corr, state, mob_hbm, spec_in, r0_in = refs[:5]
    tabs = dict(zip(MAIN, refs[5:14]))
    z_out, q_out, spec_out, pay = refs[14:18]
    st, mob, spec, field, r0, acc, sem, out_sem = refs[18:]
    kinds, lx, ly = field.shape
    sources = [(spec_in, spec), (r0_in, r0), (mob_hbm.at[:, 0, :], mob)]
    sources += [(state.at[:, 0, k, :], st.at[k]) for k in range(kinds)]
    copies = load_all(sources, kinds, sem)
    acc[...] = jnp.zeros_like(acc)
    copies[0].wait()

    @pl.loop(0, kinds)
    def _(k):
        field[k] = transform_back(spec, k, corr, field, tabs)

    z_copy = pltpu.make_async_copy(field, z_out, out_sem.at[0])
    z_copy.start()
    for copy in copies[1:]:
        copy.wait()

    @pl.loop(0, lx // 8)
    def _(i):
        row = pl.multiple_of(i * 8, 8)
        for j in range(ly // 128):
            at = (pl.ds(row, 8), slice(j * 128, (j + 1) * 128))
            move = mob[at]
            rate = time_step * move
            s = [st[(k, *at)] for k in range(kinds)]
            z = [field[(k, *at)] for k in range(kinds)]
            squares = [v * v for v in s]
            total = sum(squares)
            coupled = sum(a * b for a, b in zip(s, z))
            base = 1.0 - move + rate * (-linear_coef + 2.0 * cross_coef * total)
            square_coef = (3.0 * cubic_coef - 6.0 * cross_coef) * rate
            pull = (4.0 * cross_coef) * rate * coupled
            part = jnp.zeros((8, 128), F32)
            for k in range(kinds):
                old = r0[(k, *at)]
                image = z[k] * (base + square_coef * squares[k]) + pull * s[k] + move * old
                r0[(k, *at)] = image
                part = part + old * image
            acc[...] += part

    q_copy = pltpu.make_async_copy(r0, q_out, out_sem.at[1])
    q_copy.start()

    @pl.loop(0, kinds)
    def _(k):
        transform_out(r0, k, spec, pay, tabs, lambda k: destinations(k, kinds, gx, gy))

    spec_copy = pltpu.make_async_copy(spec, spec_out, out_sem.at[2])
    spec_copy.start()
    store_sums(pay, nrow, [lane_sum(acc[...])])
    z_copy.wait()
    q_copy.wait()
    spec_copy.wait()


def last_kernel(gx, gy, nrow, *refs):
    corr, beta_sq, state, mob_hbm, spec_in, r0_in, q_in, z_in = refs[:8]
    tabs = dict(zip(("inv_y", "inv_x", "inverse", "ends_x", "ends_y"), refs[8:13]))
    z_out, sums = refs[13:15]
    st, mob, spec, field, r0, q1, acc, sem, out_sem = refs[15:]
    kinds, lx, ly = field.shape
    sources = [(spec_in, spec), (z_in, field), (r0_in, r0), (q_in, q1), (mob_hbm.at[:, 0, :], mob)]
    sources += [(state.at[:, 0, k, :], st.at[k]) for k in range(kinds)]
    copies = load_all(sources, kinds, sem)
    acc[...] = jnp.zeros_like(acc)
    height = corr[0, nrow : nrow + 1, :] / beta_sq[0, nrow : nrow + 1, :]
    copies[0].wait()
    copies[1].wait()

    @pl.loop(0, kinds)
    def _(k):
        field[k] = transform_back(spec, k, corr, field, tabs) - height[:, :1] * field[k]

    z_copy = pltpu.make_async_copy(field, z_out, out_sem.at[0])
    z_copy.start()
    for copy in copies[2:]:
        copy.wait()

    @pl.loop(0, lx // 8)
    def _(i):
        row = pl.multiple_of(i * 8, 8)
        for j in range(ly // 128):
            at = (pl.ds(row, 8), slice(j * 128, (j + 1) * 128))
            move = mob[at]
            rate = time_step * move
            s = [st[(k, *at)] for k in range(kinds)]
            z = [field[(k, *at)] for k in range(kinds)]
            squares = [v * v for v in s]
            total = sum(squares)
            coupled = sum(a * b for a, b in zip(s, z))
            base = 1.0 - move + rate * (-linear_coef + 2.0 * cross_coef * total)
            square_coef = (3.0 * cubic_coef - 6.0 * cross_coef) * rate
            pull = (4.0 * cross_coef) * rate * coupled
            parts = [jnp.zeros((8, 128), F32)] * 4
            for k in range(kinds):
                old = r0[(k, *at)]
                basis = q1[(k, *at)] - height * old
                image = z[k] * (base + square_coef * squares[k]) + pull * s[k] + move * basis
                pairs = ((basis, basis), (basis, image), (old, image), (image, image))
                parts = [p + a * b for p, (a, b) in zip(parts, pairs)]
            for n in range(4):
                acc[n] += parts[n]

    rows = [lane_sum(acc[n]) for n in range(4)]
    for d in range(sums.shape[0]):
        for n in range(4):
            sums[d, n : n + 1, :] = rows[n]
    z_copy.wait()


def face_kernel(gx, gy, lx, ly, nrow, place, pay, *refs):
    tabs = dict(zip(FACE, refs))
    out = refs[len(FACE)]
    nx, ny = lx // 128, ly // 128
    hx, hy = lx // 2, ly // 2
    blocks = gx * gy
    dot = functools.partial(jnp.dot, precision=lax.Precision.HIGHEST, preferred_element_type=F32)
    piece = lambda start, count: jnp.concatenate([pay[:, start + j, :] for j in range(count)], axis=1)
    t_even, t_odd = piece(0, ny), piece(ny, ny)
    s_even, s_odd = piece(2 * ny, nx), piece(2 * ny + nx, nx)

    def turn(a, shift):
        shift = shift % a.shape[0]
        return a if shift == 0 else pltpu.roll(a, shift, 0)

    def group(a, shift):
        by = lax.broadcasted_iota(jnp.int32, a.shape, 0) % gy
        shift = shift % gy
        if shift == 0:
            return a
        return jnp.where(by < gy - shift, turn(a, -shift), turn(a, gy - shift))

    def circulant(coef, a, move, count):
        value = coef(0) * a
        for d in range(1, count // 2 + 1):
            near = move(a, d) if 2 * d == count else move(a, d) + move(a, -d)
            value = value + coef(d) * near
        return value

    def solve_x(jump, step):
        return circulant(lambda d: tabs["gap_x"][d : d + 1, :], jump, lambda a, d: turn(a, -d * step), gx)

    def spread(minus, plus, table, width):
        count = minus.shape[0]
        both = dot(jnp.concatenate([minus, plus], axis=0), table)
        lane = lax.broadcasted_iota(jnp.int32, (count, both.shape[1]), 1)
        return jnp.where(lane < width, -both[:count], both[count:])

    flux = solve_x(t_even - t_odd - turn(t_even + t_odd, -gy), gy)
    minus, plus = flux - turn(flux, gy), flux + turn(flux, gy)
    s_even = s_even + spread(minus[:, :hy], plus[:, :hy], tabs["cross_t"][:hy, :], hx)
    s_odd = s_odd + spread(minus[:, hy:], plus[:, hy:], tabs["cross_t"][hy:, :], hx)
    jump = s_even - s_odd - group(s_even + s_odd, 1)
    lines = dot(tabs["gather"][...], dot(jump, tabs["cos_x"][...]))
    rows = lines.shape[0] // 2
    real, imag = lines[:rows], lines[rows:]
    cosine, sine = tabs["twist"][0], tabs["twist"][1]
    turned = jnp.concatenate([real * cosine + imag * sine, imag * cosine - real * sine], axis=0)
    both = dot(turned, tabs["fourier"][...])
    waves = jnp.concatenate(
        [both[:rows, :lx] + both[rows:, lx:], both[rows:, :lx] - both[:rows, lx:]], axis=0
    )
    waves = circulant(lambda d: tabs["gap_y"][d], waves, group, gy)
    both = dot(waves, tabs["fourier"][...])
    real = both[:rows, :lx] - both[rows:, lx:]
    imag = both[:rows, lx:] + both[rows:, :lx]
    turned = jnp.concatenate([real * cosine - imag * sine, real * sine + imag * cosine], axis=0)
    flow = dot(dot(tabs["scatter"][...], turned), tabs["cos_xt"][...])
    flow_minus, flow_plus = flow - group(flow, -1), flow + group(flow, -1)
    row = lax.broadcasted_iota(jnp.int32, (gx, blocks), 0)
    col = lax.broadcasted_iota(jnp.int32, (gx, blocks), 1)
    pick = jnp.where(col == row * gy + place[0], 1.0, 0.0).astype(F32)
    chosen = dot(pick, jnp.concatenate([t_even, t_odd, flow_minus, flow_plus], axis=1))
    t_even, t_odd = chosen[:, :ly], chosen[:, ly : 2 * ly]
    minus, plus = chosen[:, 2 * ly : 2 * ly + lx], chosen[:, 2 * ly + lx :]
    t_even = t_even + spread(minus[:, :hx], plus[:, :hx], tabs["cross"][:hx, :], hy)
    t_odd = t_odd + spread(minus[:, hx:], plus[:, hx:], tabs["cross"][hx:, :], hy)
    flux = solve_x(t_even - t_odd - turn(t_even + t_odd, -1), 1)
    line = jnp.concatenate([turn(flux, 1) - flux, flux + turn(flux, 1), -minus, plus], axis=1)
    for j in range(line.shape[1] // 128):
        out[:, j, :] = line[:, j * 128 : (j + 1) * 128]
    total = jnp.sum(jnp.sum(pay[:, nrow, :], axis=0, keepdims=True), axis=1, keepdims=True)
    out[:, nrow, :] = jnp.broadcast_to(total, (gx, 128))


def finish_kernel(nrow, sums, corr, beta_in, state, z1, z2, out):
    beta_sq = beta_in[0, nrow : nrow + 1, :]
    top_left = corr[0, nrow : nrow + 1, :] / beta_sq
    beta = jnp.sqrt(beta_sq)
    total = jnp.sum(jnp.sum(sums[...], axis=0), axis=1, keepdims=True)
    total = jnp.broadcast_to(total, (8, 128))
    length_sq, cross, first, image_sq = [total[n : n + 1, :] for n in range(4)]
    length = jnp.sqrt(length_sq)
    below_first = length / beta
    top_right = first / (beta * length)
    middle_right = cross / length_sq
    bottom_sq = image_sq / length_sq - top_right * top_right - middle_right * middle_right
    first_radius = jnp.sqrt(top_left * top_left + below_first * below_first)
    first_cosine = top_left / first_radius
    first_sine = below_first / first_radius
    upper_right = first_cosine * top_right + first_sine * middle_right
    lower_right = -first_sine * top_right + first_cosine * middle_right
    lower_target = -first_sine * beta
    second_coef = lower_right * lower_target / (lower_right * lower_right + jnp.maximum(bottom_sq, 0.0))
    first_coef = (first_cosine * beta - upper_right * second_coef) / first_radius
    a = (first_coef / beta)[:, :1]
    b = (second_coef / length)[:, :1]
    for k in range(out.shape[2]):
        out[:, 0, k, :] = state[:, 0, k, :] + (a * z1[k] + b * z2[k])


def halo(state):
    def shift(cells, axis, step):
        count = lax.axis_size(axis)
        return lax.ppermute(cells, axis, [(i, (i + step) % count) for i in range(count)])

    lo = shift(state[-1:], "gx", 1)
    hi = shift(state[:1], "gx", -1)
    column = lambda cells: jnp.transpose(cells[:, 0, :, 0], (1, 0))
    left = shift(column(state[..., -1:]), "gy", 1)
    right = shift(column(state[..., :1]), "gy", -1)
    return lo, hi, jnp.stack([left, right], axis=2)


def body(gx, gy, state, mobility):
    lx, _, kinds, ly = state.shape
    main, face = make_tables(lx, ly, gx, gy)
    main = {name: jnp.asarray(table) for name, table in main.items()}
    face = {name: jnp.asarray(table) for name, table in face.items()}
    nrow = (2 * lx + 2 * ly) // 128
    width = -(-(nrow + 1) // 8) * 8
    vmem = pl.BlockSpec(memory_space=pltpu.VMEM)
    hbm = pl.BlockSpec(memory_space=pl.ANY)
    smem = pl.BlockSpec(memory_space=pltpu.SMEM)
    params = pltpu.CompilerParams(vmem_limit_bytes=VMEM_LIMIT)
    whole = jax.ShapeDtypeStruct((kinds, lx, ly), F32)
    payload = jax.ShapeDtypeStruct((gx * gy, width, 128), F32)
    full = pltpu.VMEM((kinds, lx, ly), F32)
    plane = pltpu.VMEM((lx, ly), F32)
    dma = pltpu.SemaphoreType.DMA
    place = lax.axis_index("gy").astype(jnp.int32).reshape(1)

    def faces(pay):
        pay = lax.all_to_all(pay, ("gx", "gy"), split_axis=0, concat_axis=0, tiled=True)
        fluxes = pl.pallas_call(
            functools.partial(face_kernel, gx, gy, lx, ly, nrow),
            out_shape=jax.ShapeDtypeStruct((gx, width, 128), F32),
            in_specs=[smem, vmem] + [vmem] * len(FACE),
            out_specs=vmem,
            compiler_params=params,
            name="faces",
        )(place, pay, *[face[name] for name in FACE])
        return lax.all_to_all(fluxes, "gx", split_axis=0, concat_axis=0, tiled=True)

    lo, hi, side = halo(state)
    names = ("fwd_y", "fwd_x", "inverse", "edge_x", "edge_y")
    r0, spec, pay = pl.pallas_call(
        functools.partial(start_kernel, gx, gy, nrow),
        out_shape=(whole, whole, payload),
        in_specs=[hbm, hbm, vmem, vmem, vmem] + [vmem] * len(names),
        out_specs=(hbm, hbm, vmem),
        scratch_shapes=[
            pltpu.VMEM((kinds, lx + 16, ly), F32),
            plane,
            full,
            full,
            pltpu.VMEM((8, 128), F32),
            dma((kinds + 1,)),
            dma((2,)),
        ],
        compiler_params=params,
        name="start",
    )(state, mobility, lo, hi, side, *[main[name] for name in names])
    corr_one = faces(pay)
    z1, q1, spec, pay = pl.pallas_call(
        functools.partial(middle_kernel, gx, gy, nrow),
        out_shape=(whole, whole, whole, payload),
        in_specs=[vmem, hbm, hbm, hbm, hbm] + [vmem] * len(MAIN),
        out_specs=(hbm, hbm, hbm, vmem),
        scratch_shapes=[
            full,
            plane,
            full,
            full,
            full,
            pltpu.VMEM((8, 128), F32),
            dma((kinds + 3,)),
            dma((3,)),
        ],
        compiler_params=params,
        name="middle",
    )(corr_one, state, mobility, spec, r0, *[main[name] for name in MAIN])
    corr_two = faces(pay)
    names = ("inv_y", "inv_x", "inverse", "ends_x", "ends_y")
    z2, sums = pl.pallas_call(
        functools.partial(last_kernel, gx, gy, nrow),
        out_shape=(whole, jax.ShapeDtypeStruct((gx * gy, 8, 128), F32)),
        in_specs=[vmem, vmem] + [hbm] * 6 + [vmem] * len(names),
        out_specs=(hbm, vmem),
        scratch_shapes=[
            full,
            plane,
            full,
            full,
            full,
            full,
            pltpu.VMEM((4, 8, 128), F32),
            dma((kinds + 5,)),
            dma((1,)),
        ],
        compiler_params=params,
        name="last",
    )(corr_two, corr_one, state, mobility, spec, r0, q1, z1, *[main[name] for name in names])
    sums = lax.all_to_all(sums, ("gx", "gy"), split_axis=0, concat_axis=0, tiled=True)
    step = 32
    corr_spec = pl.BlockSpec(corr_one.shape, lambda i: (0, 0, 0))
    return pl.pallas_call(
        functools.partial(finish_kernel, nrow),
        grid=(lx // step,),
        out_shape=jax.ShapeDtypeStruct(state.shape, F32),
        in_specs=[
            pl.BlockSpec(sums.shape, lambda i: (0, 0, 0)),
            corr_spec,
            corr_spec,
            pl.BlockSpec((step, 1, kinds, ly), lambda i: (i, 0, 0, 0)),
            pl.BlockSpec((kinds, step, ly), lambda i: (0, i, 0)),
            pl.BlockSpec((kinds, step, ly), lambda i: (0, i, 0)),
        ],
        out_specs=pl.BlockSpec((step, 1, kinds, ly), lambda i: (i, 0, 0, 0)),
        compiler_params=params,
        name="finish",
    )(sums, corr_two, corr_one, state, z1, z2)


def solution(mesh):
    return jax.shard_map(
        functools.partial(body, mesh.shape["gx"], mesh.shape["gy"]),
        mesh=mesh,
        in_specs=(P("gx", None, None, "gy"), P("gx", None, "gy")),
        out_specs=P("gx", None, None, "gy"),
        check_vma=False,
    )
```

```python
import functools
import math

import jax
import jax.numpy as jnp
import numpy as np
from jax import lax
from jax.experimental import pallas as pl
from jax.experimental.pallas import tpu as pltpu
from jax.sharding import PartitionSpec as P

linear_coef = 1.0
cubic_coef = 1.0
cross_coef = 1.5
gradient_coef = 200.0
time_step = 200.0
stiffness = time_step * gradient_coef

F32 = jnp.float32
BF16 = jnp.bfloat16
GRANTS = dict(edges=56, start=20, rim=8, faces=8, middle=16, last=16, finish=8)


def cosine_table(size):
    modes = np.arange(size)[:, None]
    cells = np.arange(size)[None, :]
    table = np.sqrt(2.0 / size) * np.cos(np.pi * modes * (cells + 0.5) / size)
    table[0] = np.sqrt(1.0 / size)
    values = 4.0 * np.sin(np.pi * np.arange(size) / (2 * size)) ** 2
    order = np.concatenate([np.arange(0, size, 2), np.arange(1, size, 2)])
    return table[order], values[order]


def split_const(table):
    high = table.astype(np.float32).astype(jnp.bfloat16)
    low = (table - high.astype(np.float64)).astype(np.float32).astype(jnp.bfloat16)
    return high, low


def right_const(table):
    high, low = split_const(table)
    return np.concatenate([high, low, high], axis=0)


def left_const(table):
    high, low = split_const(table)
    return np.concatenate([high, low, high], axis=1)


def make_tables(lx, ly, gx, gy):
    cos_x, value_x = cosine_table(lx)
    cos_y, value_y = cosine_table(ly)
    edge_x, edge_y = cos_x[:, 0], cos_y[:, 0]
    inverse = 1.0 / (1.0 + stiffness * (value_x[:, None] + value_y[None, :]))
    cross = edge_x[:, None] * edge_y[None, :] * inverse
    sign_x = np.where(np.arange(lx) < lx // 2, 1.0, -1.0)
    sign_y = np.where(np.arange(ly) < ly // 2, 1.0, -1.0)
    own = (edge_x[:, None] ** 2 * inverse).sum(0)
    other = (sign_x[:, None] * edge_x[:, None] ** 2 * inverse).sum(0)
    wave = np.arange(gx)
    eigen = 1.0 / stiffness + 2.0 * own[None] - 2.0 * other[None] * np.cos(2 * np.pi * wave / gx)[:, None]
    gap_x = np.stack(
        [(np.cos(2 * np.pi * wave * d / gx)[:, None] / eigen).mean(0) for d in range(gx // 2 + 1)]
    )
    total = lx * gx
    half = gx // 2 + 1
    rows = -(-half * gy // 8) * 8
    freq = gx * np.arange(lx)[None, :] + np.arange(half)[:, None]
    symbol = 1.0 + stiffness * (4.0 * np.sin(np.pi * freq / total) ** 2)[:, :, None] + stiffness * value_y
    own = (edge_y**2 / symbol).sum(-1)
    other = (sign_y * edge_y**2 / symbol).sum(-1)
    wave = np.arange(gy)
    eigen = 1.0 / stiffness + 2.0 * own[None] - 2.0 * other[None] * np.cos(2 * np.pi * wave / gy)[:, None, None]
    gap_y = np.zeros((gy // 2 + 1, 2 * rows, lx))
    for d in range(gy // 2 + 1):
        coef = (np.cos(2 * np.pi * wave * d / gy)[:, None, None] / eigen).mean(0)
        coef = np.repeat(coef, gy, axis=0)
        gap_y[d, : half * gy] = coef
        gap_y[d, rows : rows + half * gy] = coef
    cells = np.arange(lx)
    angle = 2 * np.pi * np.outer(cells, cells) / lx
    fourier = np.concatenate([np.cos(angle), np.sin(angle)], axis=1)
    twist = np.zeros((2, rows, lx))
    gather = np.zeros((2 * rows, gx * gy))
    scatter = np.zeros((gx * gy, 2 * rows))
    for q in range(half):
        theta = 2 * np.pi * q * cells / total
        weight = (1.0 if q in (0, gx // 2) else 2.0) / total
        for j in range(gy):
            twist[0, q * gy + j] = np.cos(theta)
            twist[1, q * gy + j] = np.sin(theta)
            for i in range(gx):
                phase = 2 * np.pi * q * i / gx
                gather[q * gy + j, i * gy + j] = np.cos(phase)
                gather[rows + q * gy + j, i * gy + j] = -np.sin(phase)
                scatter[i * gy + j, q * gy + j] = weight * np.cos(phase)
                scatter[i * gy + j, rows + q * gy + j] = -weight * np.sin(phase)
    single = lambda a: np.ascontiguousarray(a, dtype=np.float32)
    zero_x, zero_y = np.zeros(lx // 2), np.zeros(ly // 2)
    ends_x = np.zeros((8, lx))
    ends_x[0], ends_x[1] = (
        np.concatenate([edge_x[: lx // 2], zero_x]),
        np.concatenate([zero_x, edge_x[lx // 2 :]]),
    )
    ends_y = np.zeros((8, ly))
    ends_y[2], ends_y[3] = (
        np.concatenate([edge_y[: ly // 2], zero_y]),
        np.concatenate([zero_y, edge_y[ly // 2 :]]),
    )
    main = dict(
        fwd_ye=right_const(cos_y[: ly // 2, : ly // 2].T),
        fwd_yo=right_const(cos_y[ly // 2 :, : ly // 2].T),
        fwd_x=left_const(cos_x),
        inv_ye=right_const(cos_y[: ly // 2, : ly // 2]),
        inv_yo=right_const(cos_y[ly // 2 :, : ly // 2]),
        inv_x=left_const(cos_x.T),
        inverse=single(inverse),
        edge_x=single(np.repeat(edge_x[:, None], 128, axis=1)),
        edge_y=single(np.repeat(edge_y[None, :], 8, axis=0)),
        ends_x=single(ends_x),
        ends_y=single(ends_y),
    )
    face = dict(
        cross=single(cross),
        cross_t=single(cross.T),
        cos_x=single(cos_x),
        cos_xt=single(cos_x.T),
        gap_x=single(gap_x),
        gap_y=single(gap_y.reshape(-1, lx)),
        fourier=single(fourier),
        twist=single(twist.reshape(-1, lx)),
        gather=single(gather),
        scatter=single(scatter),
        self_x=single(np.stack([(edge_x[:, None] ** 2 * inverse)[h].sum(0) for h in np.split(np.arange(lx), 2)])),
        self_y=single(np.stack([(edge_y**2 * inverse)[:, h].sum(1) for h in np.split(np.arange(ly), 2)])),
    )
    return main, face


def packed(tables):
    arrays, places = [], []
    for kind, step in ((np.dtype(np.float32), 8), (np.dtype(jnp.bfloat16), 16)):
        strips, start = [], 0
        for name, table in tables.items():
            if table.dtype != kind:
                continue
            rows, cols = -(-table.shape[0] // step) * step, -(-table.shape[1] // 128) * 128
            wide = np.zeros((rows, cols), kind)
            wide[: table.shape[0], : table.shape[1]] = table
            for j in range(cols // 128):
                strips.append(wide[:, j * 128 : (j + 1) * 128])
                places.append((name, len(arrays), start, rows, j, cols))
                start += rows
        arrays.append(np.concatenate(strips, axis=0))
    return arrays, places


def halves(x):
    high = x.astype(BF16)
    low = (x - high.astype(F32)).astype(BF16)
    return high, low


def times_right(x, const):
    high, low = halves(x)
    return jnp.dot(jnp.concatenate([high, high, low], axis=1), const[...], preferred_element_type=F32)


def times_left(const, x):
    high, low = halves(x)
    return jnp.dot(const[...], jnp.concatenate([high, high, low], axis=0), preferred_element_type=F32)


def thirds(x):
    high = x.astype(BF16).astype(F32)
    rest = x - high
    mid = rest.astype(BF16).astype(F32)
    return high, mid, rest - mid


def outer_sum(a, b):
    ah, am, al = thirds(a)
    bh, bm, bl = thirds(b)
    left = jnp.concatenate([ah, ah, am, am, ah, al], axis=0).astype(BF16)
    right = jnp.concatenate([bh, bm, bh, bm, bl, bh], axis=0).astype(BF16)
    return lax.dot_general(left, right, (((0,), (0,)), ((), ())), preferred_element_type=F32)


def flipped(x):
    place = 127 - lax.broadcasted_iota(jnp.int32, (x.shape[0], 128), 1)
    tiles = [x[:, j * 128 : (j + 1) * 128] for j in range(x.shape[1] // 128)]
    return jnp.concatenate(
        [jnp.take_along_axis(tile, place, axis=1, mode="promise_in_bounds") for tile in tiles[::-1]], axis=1
    )


def lines_out(x, tabs):
    half = x.shape[1] // 2
    left, right = x[:, :half], flipped(x[:, half:])
    return jnp.concatenate(
        [times_right(left + right, tabs["fwd_ye"]), times_right(left - right, tabs["fwd_yo"])], axis=1
    )


def lines_back(x, tabs):
    half = x.shape[1] // 2
    even = times_right(x[:, :half], tabs["inv_ye"])
    odd = times_right(x[:, half:], tabs["inv_yo"])
    return jnp.concatenate([even + odd, flipped(even - odd)], axis=1)


def modes_out(lines, group, spec, tabs, store):
    lx, ly = spec.shape[1:]
    hat = times_left(tabs["fwd_x"], jnp.concatenate(lines, axis=1))
    for i, k in enumerate(group):
        spectrum = hat[:, i * ly : (i + 1) * ly] * tabs["inverse"][...]
        spec[k] = spectrum
        weighted = spectrum * tabs["edge_x"][:, :1]
        top = [
            jnp.sum(weighted[: lx // 2], axis=0, keepdims=True),
            jnp.sum(weighted[lx // 2 :], axis=0, keepdims=True),
        ]
        weighted = spectrum * tabs["edge_y"][:1, :]
        cols = [weighted[:, j * 128 : (j + 1) * 128] for j in range(ly // 128)]
        half = len(cols) // 2
        folded = jnp.concatenate([sum(cols[1:half], cols[0]), sum(cols[half + 1 :], cols[half])], axis=0)
        high, low = halves(folded)
        side = lax.dot_general(
            jnp.ones((8, 256), BF16),
            jnp.concatenate([high, low], axis=1),
            (((1,), (1,)), ((), ())),
            preferred_element_type=F32,
        )[:1]
        store(k, jnp.concatenate([*top, side], axis=1))


def row_piece(ref, k, start, count):
    return jnp.concatenate([ref[k, start + j : start + j + 1, :] for j in range(count)], axis=1)


def transform_back(spec, group, corrs, tabs):
    lx, ly = spec.shape[1:]
    nx, ny = lx // 128, ly // 128
    row = lax.broadcasted_iota(jnp.int32, (8, 1), 0)
    spectra = []
    for k in group:
        piece = lambda start, count: sum(row_piece(corr, k, start, count) for corr in corrs)
        a = (
            tabs["ends_x"][...]
            + jnp.where(row == 2, piece(2 * ny, nx), 0.0)
            + jnp.where(row == 3, piece(2 * ny + nx, nx), 0.0)
        )
        b = (
            tabs["ends_y"][...]
            + jnp.where(row == 0, piece(0, ny), 0.0)
            + jnp.where(row == 1, piece(ny, ny), 0.0)
        )
        spectra.append(spec[k] + tabs["inverse"][...] * outer_sum(a, b))
    lines = times_left(tabs["inv_x"], jnp.concatenate(spectra, axis=1))
    lines = jnp.concatenate([lines[:, i * ly : (i + 1) * ly] for i in range(len(group))], axis=0)
    fields = lines_back(lines, tabs)
    return [fields[i * lx : (i + 1) * lx] for i in range(len(group))]


def add_rim(field, k, rim_rows, rim_cols):
    kinds, lx, ly = field.shape
    field[k, 0:1, :] += rim_rows[k : k + 1, :]
    field[k, lx - 1 : lx, :] += rim_rows[kinds + k : kinds + k + 1, :]
    row = lax.broadcasted_iota(jnp.int32, (8, 1), 0)
    at = lax.broadcasted_iota(jnp.int32, (8, 128), 1)
    for start, source, lane in ((0, k, 0), (ly - 128, kinds + k, 127)):
        cells = jnp.where(row == 0, rim_cols[source : source + 1, :], 0.0)
        where = jnp.where((row == 0) & (at == lane), 1.0, 0.0).astype(F32)
        field[k, :, start : start + 128] += outer_sum(cells, where)


def lane_sum(x):
    return jnp.sum(x, axis=0, keepdims=True)


def store_sums(pay, start, rows):
    rest = pay.shape[1] - start
    row = lax.broadcasted_iota(jnp.int32, (rest, 128), 0)
    block = jnp.zeros((rest, 128), F32)
    for j, value in enumerate(rows):
        block = jnp.where(row == j, value, block)
    for d in range(pay.shape[0]):
        pay[d, start:, :] = block


OUT = ("fwd_ye", "fwd_yo", "fwd_x", "inverse", "edge_x", "edge_y")
BACK = ("inv_ye", "inv_yo", "inv_x", "inverse", "ends_x", "ends_y")
MAIN = OUT + ("inv_ye", "inv_yo", "inv_x", "ends_x", "ends_y")
RIM = ("cross", "cross_t", "cos_xt", "self_x", "self_y")
GROUP = 2
FACE = (
    "cross",
    "cross_t",
    "cos_x",
    "cos_xt",
    "gap_x",
    "gap_y",
    "fourier",
    "twist",
    "gather",
    "scatter",
)


def destinations(k, kinds, gx, gy):
    return [k * gy + p + kinds * gy * copy for copy in range(gx // kinds) for p in range(gy)]


def store_line(pay, places, line):
    for d in places:
        for j in range(line.shape[1] // 128):
            pay[d, j : j + 1, :] = line[:, j * 128 : (j + 1) * 128]


def edge_kernel(_, state, rows_first, rows_last, cols_first, cols_last, tiles, sem):
    kinds, lx = cols_first.shape
    last = state.shape[3] - 128
    copies = [
        pltpu.make_async_copy(state.at[0, 0], rows_first, sem.at[0]),
        pltpu.make_async_copy(state.at[lx - 1, 0], rows_last, sem.at[1]),
    ]
    for k in range(kinds):
        for n, start in enumerate((0, last)):
            copies.append(
                pltpu.make_async_copy(
                    state.at[:, 0, k, pl.ds(start, 128)],
                    tiles.at[k, :, pl.ds(n * 128, 128)],
                    sem.at[2 + 2 * k + n],
                )
            )
    for copy in copies:
        copy.start()
    row = lax.broadcasted_iota(jnp.int32, (8, 256), 0)
    lane = lax.broadcasted_iota(jnp.int32, (8, 256), 1)
    pick = jnp.where(((row == 0) & (lane == 0)) | ((row == 1) & (lane == 255)), 1.0, 0.0)
    pick = jnp.concatenate([pick] * 3, axis=1).astype(BF16)
    for copy in copies[2:]:
        copy.wait()
    for k in range(kinds):
        cells = jnp.concatenate(thirds(tiles[k]), axis=1).astype(BF16)
        ends = lax.dot_general(pick, cells, (((1,), (1,)), ((), ())), preferred_element_type=F32)
        cols_first[k : k + 1, :] = ends[0:1]
        cols_last[k : k + 1, :] = ends[1:2]
    for copy in copies[:2]:
        copy.wait()


def start_kernel(parts, names, places, state, mob_hbm, *refs):
    packs, refs = refs[:2], refs[2:]
    count = len(names)
    tabs = dict(zip(names, refs[:count]))
    cells, mob, r0, spec, line_out = refs[count : count + 5]
    st, field, lines, base, sem, tab_sem = refs[count + 5 :]
    lx, kinds, ly = field.shape
    size = lx // parts
    copies = [
        pltpu.make_async_copy(state.at[pl.ds(c * size, size), 0], st.at[pl.ds(1 + c * size, size)], sem.at[c])
        for c in range(parts)
    ]
    mob_copy = pltpu.make_async_copy(mob_hbm.at[:, 0, :], mob, sem.at[parts])
    mob_copy.start()
    for copy in copies:
        copy.start()
    loads = {name: [] for name in names}
    for n, (name, which, start, rows, j, _) in enumerate(places):
        loads[name].append(
            pltpu.make_async_copy(
                packs[which].at[pl.ds(start, rows)], tabs[name].at[:, pl.ds(j * 128, 128)], tab_sem.at[n]
            )
        )
    for name in names:
        for copy in loads[name]:
            copy.start()
    lane = lax.broadcasted_iota(jnp.int32, (kinds, ly), 1)

    def force(start):
        for i in range(size // 8):
            row = pl.multiple_of(start + i * 8, 8)
            total = sum(st[pl.ds(row + 1, 8), k, :] ** 2 for k in range(kinds))
            base[i] = -linear_coef + 2.0 * cross_coef * total
            rates = time_step * mob[pl.ds(row, 8), :]
            for j in range(8):
                mid = st[row + 1 + j]
                left = jnp.where(lane == 0, mid, pltpu.roll(mid, 1, 1))
                right = jnp.where(lane == ly - 1, mid, pltpu.roll(mid, ly - 1, 1))
                lap = (st[row + j] + st[row + 2 + j]) + (left + right) - 4.0 * mid
                react = mid * (base[i, j : j + 1, :] + (cubic_coef - 2.0 * cross_coef) * (mid * mid))
                field[row + j] = rates[j : j + 1, :] * (gradient_coef * lap - react)

    def rows_out(start):
        rows = field[pl.ds(start, size)].reshape(size * kinds, ly)
        lines[pl.ds(start, size)] = lines_out(rows, tabs).reshape(size, kinds, ly)

    mob_copy.wait()
    copies[0].wait()
    copies[1].wait()
    st[0] = st[1]
    force(0)
    for copy in copies[2:]:
        copy.wait()
    st[lx + 1] = st[lx]
    for name in OUT:
        for copy in loads[name]:
            copy.wait()

    @pl.loop(1, parts)
    def _(c):
        rows_out(pl.multiple_of((c - 1) * size, size))
        force(pl.multiple_of(c * size, size))

    rows_out(lx - size)

    @pl.loop(0, lx // 8)
    def _(i):
        row = pl.multiple_of(i * 8, 8)
        for k in range(kinds):
            cells[k, pl.ds(row, 8), :] = st[pl.ds(row + 1, 8), k, :]
            r0[k, pl.ds(row, 8), :] = field[pl.ds(row, 8), k, :]

    for k in range(0, kinds, GROUP):
        group = list(range(k, k + GROUP))
        modes_out(
            [lines[:, g, :] for g in group], group, spec, tabs, lambda g, line: store_line(line_out, [g], line)
        )
    for name in names:
        for copy in loads[name]:
            if name not in OUT:
                copy.wait()


def rim_kernel(gx, gy, lx, ly, *refs):
    line, lo, hi, near_left, near_right, own_left, own_right, st, mob = refs[:9]
    names = RIM + ("fwd_ye", "fwd_yo")
    tabs = dict(zip(names, refs[9 : 9 + len(names)]))
    pay, corr, rows_out, cols_out = refs[9 + len(names) :]
    kinds = line.shape[0]
    nx, ny = lx // 128, ly // 128
    hx, hy = lx // 2, ly // 2
    dot = functools.partial(jnp.dot, precision=lax.Precision.HIGHEST, preferred_element_type=F32)

    def column(start, lane):
        where = jnp.where(lax.broadcasted_iota(jnp.int32, (8, 128), 1) == lane, 1.0, 0.0).astype(F32)
        return lax.dot_general(
            where,
            mob[:, start : start + 128],
            (((1,), (1,)), ((), ())),
            precision=lax.Precision.HIGHEST,
            preferred_element_type=F32,
        )

    top = stiffness * mob[0:1, :] * (lo[...] - st[:, 0, :])
    bottom = stiffness * mob[lx - 1 : lx, :] * (hi[...] - st[:, lx - 1, :])
    left = stiffness * column(0, 0) * (near_left[...] - own_left[...])
    right = stiffness * column(ly - 128, 127) * (near_right[...] - own_right[...])
    rows = jnp.concatenate([top, bottom], axis=0)
    cols = jnp.concatenate([left, right], axis=0)
    rows_out[...] = rows
    cols_out[...] = cols
    rows = lines_out(rows, tabs)
    cols = dot(cols, tabs["cos_xt"][...])
    row_even, row_odd = rows[:kinds] + rows[kinds:], rows[:kinds] - rows[kinds:]
    col_even, col_odd = cols[:kinds] + cols[kinds:], cols[:kinds] - cols[kinds:]

    def spread(even, odd, table, width):
        both = dot(jnp.concatenate([even, odd], axis=0), table)
        lane = lax.broadcasted_iota(jnp.int32, (kinds, both.shape[1]), 1)
        return jnp.where(lane < width, both[:kinds], both[kinds:])

    add = [
        tabs["self_x"][0:1, :] * row_even + spread(col_even[:, :hx], col_odd[:, :hx], tabs["cross"][:hx, :], hy),
        tabs["self_x"][1:2, :] * row_odd + spread(col_even[:, hx:], col_odd[:, hx:], tabs["cross"][hx:, :], hy),
        tabs["self_y"][0:1, :] * col_even
        + spread(row_even[:, :hy], row_odd[:, :hy], tabs["cross_t"][:hy, :], hx),
        tabs["self_y"][1:2, :] * col_odd
        + spread(row_even[:, hy:], row_odd[:, hy:], tabs["cross_t"][hy:, :], hx),
    ]
    add = jnp.concatenate(add, axis=1)
    share = jnp.concatenate([row_even, row_odd, col_even, col_odd], axis=1)
    count = 2 * (nx + ny)
    for j in range(corr.shape[1]):
        if j < count:
            corr[:, j, :] = share[:, j * 128 : (j + 1) * 128]
            value = line[:, j, :] + add[:, j * 128 : (j + 1) * 128]
        else:
            corr[:, j, :] = jnp.zeros((kinds, 128), F32)
            value = jnp.zeros((kinds, 128), F32)
        for copy in range(gx // kinds):
            for p in range(gy):
                pay[pl.ds(copy * kinds * gy + p, kinds, stride=gy), j, :] = value


def middle_kernel(gx, gy, nrow, *refs):
    corr, rim, rim_rows, rim_cols, st, mob, _, _ = refs[:8]
    tabs = dict(zip(MAIN, refs[8 : 8 + len(MAIN)]))
    r0, spec, field, q1, pay, acc = refs[8 + len(MAIN) :]
    kinds, lx, ly = r0.shape
    acc[...] = jnp.zeros_like(acc)
    for k in range(0, kinds, GROUP):
        group = list(range(k, k + GROUP))
        for g, cells in zip(group, transform_back(spec, group, (corr, rim), tabs)):
            field[g] = cells
            add_rim(r0, g, rim_rows, rim_cols)

    @pl.loop(0, lx // 8)
    def _(i):
        row = pl.multiple_of(i * 8, 8)
        for j in range(ly // 128):
            lanes = slice(j * 128, (j + 1) * 128)
            move = mob[pl.ds(row, 8), lanes]
            rate = time_step * move
            s = [st[k, pl.ds(row, 8), lanes] for k in range(kinds)]
            z = [field[k, pl.ds(row, 8), lanes] for k in range(kinds)]
            squares = [v * v for v in s]
            total = sum(squares)
            coupled = sum(a * b for a, b in zip(s, z))
            base = 1.0 - move + rate * (-linear_coef + 2.0 * cross_coef * total)
            square_coef = (3.0 * cubic_coef - 6.0 * cross_coef) * rate
            pull = (4.0 * cross_coef) * rate * coupled
            parts = [jnp.zeros((8, 128), F32)] * 2
            for k in range(kinds):
                old = r0[k, pl.ds(row, 8), lanes]
                image = z[k] * (base + square_coef * squares[k]) + pull * s[k] + move * old
                q1[k, pl.ds(row, 8), lanes] = image
                pairs = ((old, old), (old, image))
                parts = [p + a * b for p, (a, b) in zip(parts, pairs)]
            for n in range(2):
                acc[n] += parts[n]

    for k in range(0, kinds, GROUP):
        group = list(range(k, k + GROUP))
        lines = lines_out(jnp.concatenate([q1[g] for g in group], axis=0), tabs)
        modes_out(
            [lines[i * lx : (i + 1) * lx] for i in range(GROUP)],
            group,
            spec,
            tabs,
            lambda g, line: store_line(pay, destinations(g, kinds, gx, gy), line),
        )
    store_sums(pay, nrow, [lane_sum(acc[n]) for n in range(2)])


def last_kernel(nrow, *refs):
    corr, st, mob, spec, r0, q1, z1 = refs[:7]
    tabs = dict(zip(BACK, refs[7 : 7 + len(BACK)]))
    field, sums, acc = refs[7 + len(BACK) :]
    kinds, lx, ly = r0.shape
    acc[...] = jnp.zeros_like(acc)
    height = corr[0, nrow + 1 : nrow + 2, :] / corr[0, nrow : nrow + 1, :]
    for k in range(0, kinds, GROUP):
        group = list(range(k, k + GROUP))
        for g, cells in zip(group, transform_back(spec, group, (corr,), tabs)):
            field[g] = cells - height[:, :1] * z1[g]

    @pl.loop(0, lx // 8)
    def _(i):
        row = pl.multiple_of(i * 8, 8)
        for j in range(ly // 128):
            lanes = slice(j * 128, (j + 1) * 128)
            move = mob[pl.ds(row, 8), lanes]
            rate = time_step * move
            s = [st[k, pl.ds(row, 8), lanes] for k in range(kinds)]
            z = [field[k, pl.ds(row, 8), lanes] for k in range(kinds)]
            squares = [v * v for v in s]
            total = sum(squares)
            coupled = sum(a * b for a, b in zip(s, z))
            base = 1.0 - move + rate * (-linear_coef + 2.0 * cross_coef * total)
            square_coef = (3.0 * cubic_coef - 6.0 * cross_coef) * rate
            pull = (4.0 * cross_coef) * rate * coupled
            parts = [jnp.zeros((8, 128), F32)] * 4
            for k in range(kinds):
                old = r0[k, pl.ds(row, 8), lanes]
                basis = q1[k, pl.ds(row, 8), lanes] - height * old
                image = z[k] * (base + square_coef * squares[k]) + pull * s[k] + move * basis
                pairs = ((basis, basis), (basis, image), (old, image), (image, image))
                parts = [p + a * b for p, (a, b) in zip(parts, pairs)]
            for n in range(4):
                acc[n] += parts[n]

    store_sums(sums, 0, [lane_sum(acc[n]) for n in range(4)])


def face_kernel(gx, gy, lx, ly, nrow, place, pay, *refs):
    tabs = dict(zip(FACE, refs))
    out = refs[len(FACE)]
    nx, ny = lx // 128, ly // 128
    hx, hy = lx // 2, ly // 2
    blocks = gx * gy
    dot = functools.partial(jnp.dot, precision=lax.Precision.HIGHEST, preferred_element_type=F32)
    piece = lambda start, count: jnp.concatenate([pay[:, start + j, :] for j in range(count)], axis=1)
    t_even, t_odd = piece(0, ny), piece(ny, ny)
    s_even, s_odd = piece(2 * ny, nx), piece(2 * ny + nx, nx)

    def turn(a, shift):
        shift = shift % a.shape[0]
        return a if shift == 0 else pltpu.roll(a, shift, 0)

    def group(a, shift):
        by = lax.broadcasted_iota(jnp.int32, a.shape, 0) % gy
        shift = shift % gy
        if shift == 0:
            return a
        return jnp.where(by < gy - shift, turn(a, -shift), turn(a, gy - shift))

    def circulant(coef, a, move, count):
        value = coef(0) * a
        for d in range(1, count // 2 + 1):
            near = move(a, d) if 2 * d == count else move(a, d) + move(a, -d)
            value = value + coef(d) * near
        return value

    def solve_x(jump, step):
        return circulant(lambda d: tabs["gap_x"][d : d + 1, :], jump, lambda a, d: turn(a, -d * step), gx)

    def spread(minus, plus, table, width):
        count = minus.shape[0]
        both = dot(jnp.concatenate([minus, plus], axis=0), table)
        lane = lax.broadcasted_iota(jnp.int32, (count, both.shape[1]), 1)
        return jnp.where(lane < width, -both[:count], both[count:])

    flux = solve_x(t_even - t_odd - turn(t_even + t_odd, -gy), gy)
    minus, plus = flux - turn(flux, gy), flux + turn(flux, gy)
    s_even = s_even + spread(minus[:, :hy], plus[:, :hy], tabs["cross_t"][:hy, :], hx)
    s_odd = s_odd + spread(minus[:, hy:], plus[:, hy:], tabs["cross_t"][hy:, :], hx)
    jump = s_even - s_odd - group(s_even + s_odd, 1)
    lines = dot(tabs["gather"][:, :blocks], dot(jump, tabs["cos_x"][...]))
    rows = lines.shape[0] // 2
    real, imag = lines[:rows], lines[rows:]
    cosine, sine = tabs["twist"][:rows, :], tabs["twist"][rows:, :]
    turned = jnp.concatenate([real * cosine + imag * sine, imag * cosine - real * sine], axis=0)
    both = dot(turned, tabs["fourier"][...])
    waves = jnp.concatenate(
        [both[:rows, :lx] + both[rows:, lx:], both[rows:, :lx] - both[:rows, lx:]], axis=0
    )
    waves = circulant(lambda d: tabs["gap_y"][2 * rows * d : 2 * rows * (d + 1), :], waves, group, gy)
    both = dot(waves, tabs["fourier"][...])
    real = both[:rows, :lx] - both[rows:, lx:]
    imag = both[:rows, lx:] + both[rows:, :lx]
    turned = jnp.concatenate([real * cosine - imag * sine, real * sine + imag * cosine], axis=0)
    flow = dot(dot(tabs["scatter"][:, : 2 * rows], turned), tabs["cos_xt"][...])
    flow_minus, flow_plus = flow - group(flow, -1), flow + group(flow, -1)
    row = lax.broadcasted_iota(jnp.int32, (gx, blocks), 0)
    col = lax.broadcasted_iota(jnp.int32, (gx, blocks), 1)
    pick = jnp.where(col == row * gy + place[0], 1.0, 0.0).astype(F32)
    chosen = dot(pick, jnp.concatenate([t_even, t_odd, flow_minus, flow_plus], axis=1))
    t_even, t_odd = chosen[:, :ly], chosen[:, ly : 2 * ly]
    minus, plus = chosen[:, 2 * ly : 2 * ly + lx], chosen[:, 2 * ly + lx :]
    t_even = t_even + spread(minus[:, :hx], plus[:, :hx], tabs["cross"][:hx, :], hy)
    t_odd = t_odd + spread(minus[:, hx:], plus[:, hx:], tabs["cross"][hx:, :], hy)
    flux = solve_x(t_even - t_odd - turn(t_even + t_odd, -1), 1)
    line = jnp.concatenate([turn(flux, 1) - flux, flux + turn(flux, 1), -minus, plus], axis=1)
    for j in range(line.shape[1] // 128):
        out[:, j, :] = line[:, j * 128 : (j + 1) * 128]
    for n in range(nrow, nrow + 2):
        total = jnp.sum(jnp.sum(pay[:, n, :], axis=0, keepdims=True), axis=1, keepdims=True)
        out[:, n, :] = jnp.broadcast_to(total, (gx, 128))


def finish_kernel(nrow, sums, corr, st, z1, z2, out_hbm, out, sem):
    beta_sq = corr[0, nrow : nrow + 1, :]
    top_left = corr[0, nrow + 1 : nrow + 2, :] / beta_sq
    beta = jnp.sqrt(beta_sq)
    total = jnp.sum(jnp.sum(sums[...], axis=0), axis=1, keepdims=True)
    total = jnp.broadcast_to(total, (8, 128))
    length_sq, cross, first, image_sq = [total[n : n + 1, :] for n in range(4)]
    length = jnp.sqrt(length_sq)
    below_first = length / beta
    top_right = first / (beta * length)
    middle_right = cross / length_sq
    bottom_sq = image_sq / length_sq - top_right * top_right - middle_right * middle_right
    first_radius = jnp.sqrt(top_left * top_left + below_first * below_first)
    first_cosine = top_left / first_radius
    first_sine = below_first / first_radius
    upper_right = first_cosine * top_right + first_sine * middle_right
    lower_right = -first_sine * top_right + first_cosine * middle_right
    lower_target = -first_sine * beta
    second_coef = lower_right * lower_target / (lower_right * lower_right + jnp.maximum(bottom_sq, 0.0))
    first_coef = (first_cosine * beta - upper_right * second_coef) / first_radius
    a = (first_coef / beta)[:, :1]
    b = (second_coef / length)[:, :1]
    lx, kinds, ly = out.shape
    parts = sem.shape[0]
    size = lx // parts
    copies = []
    for c in range(parts):

        @pl.loop(c * size // 8, (c + 1) * size // 8)
        def _(i):
            row = pl.multiple_of(i * 8, 8)
            for k in range(kinds):
                update = a * z1[k, pl.ds(row, 8), :] + b * z2[k, pl.ds(row, 8), :]
                out[pl.ds(row, 8), k, :] = st[k, pl.ds(row, 8), :] + update

        copies.append(
            pltpu.make_async_copy(
                out.at[pl.ds(c * size, size)], out_hbm.at[pl.ds(c * size, size), 0], sem.at[c]
            )
        )
        copies[-1].start()
    for copy in copies:
        copy.wait()


def halo(rows_first, rows_last, cols_first, cols_last):
    def shift(cells, axis, step):
        count = lax.axis_size(axis)
        return lax.ppermute(cells, axis, [(i, (i + step) % count) for i in range(count)])

    return (
        shift(rows_last, "gx", 1),
        shift(rows_first, "gx", -1),
        shift(cols_last, "gy", 1),
        shift(cols_first, "gy", -1),
    )


def body(gx, gy, state, mobility):
    lx, _, kinds, ly = state.shape
    main, face = make_tables(lx, ly, gx, gy)
    tables = {**main, **face}
    names = list(OUT) + [name for name in tables if name not in OUT]
    packs, places = packed(tables)
    pick = lambda some: [tables[name] for name in some]
    rest = lambda some: [tables[name] for name in names if name not in some]
    nrow = (2 * lx + 2 * ly) // 128
    width = -(-(nrow + 2) // 8) * 8
    vmem = pl.BlockSpec(memory_space=pltpu.VMEM)
    hbm = pl.BlockSpec(memory_space=pl.ANY)
    smem = pl.BlockSpec(memory_space=pltpu.SMEM)
    grant = lambda mib: pltpu.CompilerParams(vmem_limit_bytes=mib * 1024 * 1024)
    array = lambda *shape: jax.ShapeDtypeStruct(shape, F32)
    whole = array(kinds, lx, ly)
    payload = array(gx * gy, width, 128)
    dma = pltpu.SemaphoreType.DMA
    place = lax.axis_index("gy").astype(jnp.int32).reshape(1)

    def kernel(function, name, inputs, keep, **options):
        count = len(inputs)

        def run(*refs):
            function(*refs[:count], *refs[count + len(keep) :])

        specs = [smem if x is place else vmem for x in inputs] + [vmem] * len(keep)
        return pl.pallas_call(
            run, in_specs=specs, compiler_params=grant(GRANTS[name]), name=name, **options
        )(*inputs, *keep)

    def faces(pay, keep):
        pay = lax.all_to_all(pay, ("gx", "gy"), split_axis=0, concat_axis=0, tiled=True)
        fluxes = kernel(
            functools.partial(face_kernel, gx, gy, lx, ly, nrow),
            "faces",
            [place, pay, *pick(FACE)],
            keep + rest(FACE),
            out_shape=array(gx, width, 128),
            out_specs=vmem,
        )
        return lax.all_to_all(fluxes, "gx", split_axis=0, concat_axis=0, tiled=True)

    rows, cols = array(kinds, ly), array(kinds, lx)
    edges = pl.pallas_call(
        edge_kernel,
        out_shape=(rows, rows, cols, cols),
        in_specs=[smem, hbm],
        out_specs=(vmem,) * 4,
        scratch_shapes=[pltpu.VMEM((kinds, lx, 256), F32), dma((2 + 2 * kinds,))],
        compiler_params=grant(GRANTS["edges"]),
        name="edges",
    )(place, state)
    near = halo(*edges)
    parts = 4
    wide = {name: (count, width) for name, _, _, count, _, width in places}
    shapes = [jax.ShapeDtypeStruct(wide[name], tables[name].dtype) for name in names]
    outs = pl.pallas_call(
        functools.partial(start_kernel, parts, names, places),
        out_shape=(*shapes, whole, array(lx, ly), whole, whole, array(kinds, width, 128)),
        in_specs=[hbm] * 4,
        out_specs=(vmem,) * (5 + len(names)),
        scratch_shapes=[
            pltpu.VMEM((lx + 2, kinds, ly), F32),
            pltpu.VMEM((lx, kinds, ly), F32),
            pltpu.VMEM((lx, kinds, ly), F32),
            pltpu.VMEM((lx // parts // 8, 8, ly), F32),
            dma((parts + 1,)),
            dma((len(places),)),
        ],
        compiler_params=grant(GRANTS["start"]),
        cost_estimate=pl.CostEstimate(flops=10**10, bytes_accessed=2 * 10**7, transcendentals=0),
        name="start",
    )(state, mobility, *[jnp.asarray(pack) for pack in packs])
    tables = dict(zip(names, outs))
    st, mob, r0, spec, line = outs[len(names) :]
    some = RIM + ("fwd_ye", "fwd_yo")
    pay, rim, rim_rows, rim_cols = kernel(
        functools.partial(rim_kernel, gx, gy, lx, ly),
        "rim",
        [line, *near, *edges[2:], st, mob, *pick(some)],
        [r0, spec] + rest(some),
        out_shape=(payload, array(kinds, width, 128), array(2 * kinds, ly), array(2 * kinds, lx)),
        out_specs=(vmem,) * 4,
    )
    corr = faces(pay, [st, mob, r0, spec, rim, rim_rows, rim_cols])
    r0, spec, z1, q1, pay = kernel(
        functools.partial(middle_kernel, gx, gy, nrow),
        "middle",
        [corr, rim, rim_rows, rim_cols, st, mob, r0, spec, *pick(MAIN)],
        rest(MAIN),
        out_shape=(whole, whole, whole, whole, payload),
        out_specs=(vmem,) * 5,
        scratch_shapes=[pltpu.VMEM((2, 8, 128), F32)],
        input_output_aliases={6: 0, 7: 1},
    )
    corr = faces(pay, [st, mob, r0, spec, z1, q1])
    z2, sums = kernel(
        functools.partial(last_kernel, nrow),
        "last",
        [corr, st, mob, spec, r0, q1, z1, *pick(BACK)],
        [],
        out_shape=(whole, array(gx * gy, 8, 128)),
        out_specs=(vmem,) * 2,
        scratch_shapes=[pltpu.VMEM((4, 8, 128), F32)],
    )
    sums = lax.all_to_all(sums, ("gx", "gy"), split_axis=0, concat_axis=0, tiled=True)
    return kernel(
        functools.partial(finish_kernel, nrow),
        "finish",
        [sums, corr, st, z1, z2],
        [],
        out_shape=jax.ShapeDtypeStruct(state.shape, F32),
        out_specs=hbm,
        scratch_shapes=[pltpu.VMEM((lx, kinds, ly), F32), dma((4,))],
    )


def solution(mesh):
    return jax.shard_map(
        functools.partial(body, mesh.shape["gx"], mesh.shape["gy"]),
        mesh=mesh,
        in_specs=(P("gx", None, None, "gy"), P("gx", None, "gy")),
        out_specs=P("gx", None, None, "gy"),
        check_vma=False,
    )
```

```python
import functools
import math

import jax
import jax.numpy as jnp
import numpy as np
from jax import lax
from jax.experimental import pallas as pl
from jax.experimental.pallas import tpu as pltpu
from jax.sharding import PartitionSpec as P

linear_coef = 1.0
cubic_coef = 1.0
cross_coef = 1.5
gradient_coef = 200.0
time_step = 200.0
stiffness = time_step * gradient_coef

F32 = jnp.float32
BF16 = jnp.bfloat16
GRANTS = dict(edges=4, start=13, rim=4, faces=4, middle=10, last=10, finish=6)


def cosine_table(size):
    modes = np.arange(size)[:, None]
    cells = np.arange(size)[None, :]
    table = np.sqrt(2.0 / size) * np.cos(np.pi * modes * (cells + 0.5) / size)
    table[0] = np.sqrt(1.0 / size)
    values = 4.0 * np.sin(np.pi * np.arange(size) / (2 * size)) ** 2
    order = np.concatenate([np.arange(0, size, 2), np.arange(1, size, 2)])
    return table[order], values[order]


def split_const(table):
    high = table.astype(np.float32).astype(jnp.bfloat16)
    low = (table - high.astype(np.float64)).astype(np.float32).astype(jnp.bfloat16)
    return high, low


def right_const(table):
    high, low = split_const(table)
    return np.concatenate([high, low, high], axis=0)


def left_const(table):
    high, low = split_const(table)
    return np.concatenate([high, low, high], axis=1)


def make_tables(lx, ly, gx, gy):
    cos_x, value_x = cosine_table(lx)
    cos_y, value_y = cosine_table(ly)
    edge_x, edge_y = cos_x[:, 0], cos_y[:, 0]
    inverse = 1.0 / (1.0 + stiffness * (value_x[:, None] + value_y[None, :]))
    cross = edge_x[:, None] * edge_y[None, :] * inverse
    sign_x = np.where(np.arange(lx) < lx // 2, 1.0, -1.0)
    sign_y = np.where(np.arange(ly) < ly // 2, 1.0, -1.0)
    own = (edge_x[:, None] ** 2 * inverse).sum(0)
    other = (sign_x[:, None] * edge_x[:, None] ** 2 * inverse).sum(0)
    wave = np.arange(gx)
    eigen = 1.0 / stiffness + 2.0 * own[None] - 2.0 * other[None] * np.cos(2 * np.pi * wave / gx)[:, None]
    gap_x = np.stack(
        [(np.cos(2 * np.pi * wave * d / gx)[:, None] / eigen).mean(0) for d in range(gx // 2 + 1)]
    )
    total = lx * gx
    half = gx // 2 + 1
    rows = -(-half * gy // 8) * 8
    freq = gx * np.arange(lx)[None, :] + np.arange(half)[:, None]
    symbol = 1.0 + stiffness * (4.0 * np.sin(np.pi * freq / total) ** 2)[:, :, None] + stiffness * value_y
    own = (edge_y**2 / symbol).sum(-1)
    other = (sign_y * edge_y**2 / symbol).sum(-1)
    wave = np.arange(gy)
    eigen = 1.0 / stiffness + 2.0 * own[None] - 2.0 * other[None] * np.cos(2 * np.pi * wave / gy)[:, None, None]
    gap_y = np.zeros((gy // 2 + 1, 2 * rows, lx))
    for d in range(gy // 2 + 1):
        coef = (np.cos(2 * np.pi * wave * d / gy)[:, None, None] / eigen).mean(0)
        coef = np.repeat(coef, gy, axis=0)
        gap_y[d, : half * gy] = coef
        gap_y[d, rows : rows + half * gy] = coef
    cells = np.arange(lx)
    angle = 2 * np.pi * np.outer(cells, cells) / lx
    fourier = np.concatenate([np.cos(angle), np.sin(angle)], axis=1)
    twist = np.zeros((2, rows, lx))
    gather = np.zeros((2 * rows, gx * gy))
    scatter = np.zeros((gx * gy, 2 * rows))
    for q in range(half):
        theta = 2 * np.pi * q * cells / total
        weight = (1.0 if q in (0, gx // 2) else 2.0) / total
        for j in range(gy):
            twist[0, q * gy + j] = np.cos(theta)
            twist[1, q * gy + j] = np.sin(theta)
            for i in range(gx):
                phase = 2 * np.pi * q * i / gx
                gather[q * gy + j, i * gy + j] = np.cos(phase)
                gather[rows + q * gy + j, i * gy + j] = -np.sin(phase)
                scatter[i * gy + j, q * gy + j] = weight * np.cos(phase)
                scatter[i * gy + j, rows + q * gy + j] = -weight * np.sin(phase)
    single = lambda a: np.ascontiguousarray(a, dtype=np.float32)
    main = dict(
        fwd_ye=right_const(cos_y[: ly // 2, : ly // 2].T),
        fwd_yo=right_const(cos_y[ly // 2 :, : ly // 2].T),
        fwd_x=left_const(cos_x),
        inv_ye=right_const(cos_y[: ly // 2, : ly // 2]),
        inv_yo=right_const(cos_y[ly // 2 :, : ly // 2]),
        inv_x=left_const(cos_x.T),
        inverse=single(inverse),
        edge_x=single(np.repeat(edge_x[:, None], 128, axis=1)),
        edge_y=single(np.repeat(edge_y[None, :], 8, axis=0)),
        pull_x=single(inverse * edge_x[:, None]),
        pull_y=single(inverse * edge_y[None, :]),
    )
    face = dict(
        cross_e=right_const(cross[: lx // 2]),
        cross_o=right_const(cross[lx // 2 :]),
        cross_te=right_const(cross.T[: ly // 2]),
        cross_to=right_const(cross.T[ly // 2 :]),
        cos_x=right_const(cos_x),
        cos_xt=right_const(cos_x.T),
        gap_x=single(gap_x),
        gap_y=single(gap_y.reshape(-1, lx)),
        fourier=right_const(fourier),
        twist=single(twist.reshape(-1, lx)),
        gather=left_const(gather),
        scatter=left_const(scatter),
        self_x=single(np.stack([(edge_x[:, None] ** 2 * inverse)[h].sum(0) for h in np.split(np.arange(lx), 2)])),
        self_y=single(np.stack([(edge_y**2 * inverse)[:, h].sum(1) for h in np.split(np.arange(ly), 2)])),
    )
    return main, face


def packed(tables, strip):
    arrays, places = [], []
    for kind, step in ((np.dtype(jnp.bfloat16), 16), (np.dtype(np.float32), 8)):
        strips, start = [], 0
        for name, table in tables.items():
            if table.dtype != kind:
                continue
            rows, cols = -(-table.shape[0] // step) * step, -(-table.shape[1] // strip) * strip
            wide = np.zeros((rows, cols), kind)
            wide[: table.shape[0], : table.shape[1]] = table
            for j in range(0, cols, strip):
                strips.append(wide[:, j : j + strip])
                places.append((name, len(arrays), start, *table.shape))
                start += rows
        arrays.append(np.concatenate(strips, axis=0))
    return arrays, places


class Table:
    def __init__(self, ref, starts, rows, cols):
        self.ref, self.starts, self.shape = ref, starts, (rows, cols)

    def __getitem__(self, index):
        index = (slice(None), slice(None)) if index is Ellipsis else index
        (top, bottom, _), (left, right, _) = [part.indices(size) for part, size in zip(index, self.shape)]
        strip = self.ref.shape[1]
        pieces = []
        for j, start in enumerate(self.starts):
            low, high = max(left - j * strip, 0), min(right - j * strip, strip)
            if low < high:
                pieces.append(self.ref[start + top : start + bottom, low:high])
        return pieces[0] if len(pieces) == 1 else jnp.concatenate(pieces, axis=1)


def unpacked(refs, places):
    starts, found = {}, {}
    for name, which, start, rows, cols in places:
        starts.setdefault(name, []).append(start)
        found[name] = Table(refs[which], starts[name], rows, cols)
    return found


def halves(x):
    high = x.astype(BF16)
    low = (x - high.astype(F32)).astype(BF16)
    return high, low


def times_right(x, const):
    high, low = halves(x)
    return jnp.dot(jnp.concatenate([high, high, low], axis=1), const[...], preferred_element_type=F32)


def times_left(const, x):
    high, low = halves(x)
    return jnp.dot(const[...], jnp.concatenate([high, high, low], axis=0), preferred_element_type=F32)


def thirds(x):
    high = x.astype(BF16).astype(F32)
    rest = x - high
    mid = rest.astype(BF16).astype(F32)
    return high, mid, rest - mid


def outer_sum(a, b):
    ah, am, al = thirds(a)
    bh, bm, bl = thirds(b)
    left = jnp.concatenate([ah, ah, am, am, ah, al], axis=0).astype(BF16)
    right = jnp.concatenate([bh, bm, bh, bm, bl, bh], axis=0).astype(BF16)
    return lax.dot_general(left, right, (((0,), (0,)), ((), ())), preferred_element_type=F32)


def flipped(x):
    place = 127 - lax.broadcasted_iota(jnp.int32, (x.shape[0], 128), 1)
    tiles = [x[:, j * 128 : (j + 1) * 128] for j in range(x.shape[1] // 128)]
    return jnp.concatenate(
        [jnp.take_along_axis(tile, place, axis=1, mode="promise_in_bounds") for tile in tiles[::-1]], axis=1
    )


def lines_out(x, tabs):
    half = x.shape[1] // 2
    left, right = x[:, :half], flipped(x[:, half:])
    return jnp.concatenate(
        [times_right(left + right, tabs["fwd_ye"]), times_right(left - right, tabs["fwd_yo"])], axis=1
    )


def lines_back(x, tabs):
    half = x.shape[1] // 2
    even = times_right(x[:, :half], tabs["inv_ye"])
    odd = times_right(x[:, half:], tabs["inv_yo"])
    return jnp.concatenate([even + odd, flipped(even - odd)], axis=1)


def modes_out(lines, group, spec, tabs, store):
    lx, ly = spec.shape[1:]
    hat = times_left(tabs["fwd_x"], jnp.concatenate(lines, axis=1))
    for i, k in enumerate(group):
        spectrum = hat[:, i * ly : (i + 1) * ly] * tabs["inverse"][...]
        spec[k] = spectrum
        weighted = spectrum * tabs["edge_x"][:, :1]
        top = [
            jnp.sum(weighted[: lx // 2], axis=0, keepdims=True),
            jnp.sum(weighted[lx // 2 :], axis=0, keepdims=True),
        ]
        weighted = spectrum * tabs["edge_y"][:1, :]
        cols = [weighted[:, j * 128 : (j + 1) * 128] for j in range(ly // 128)]
        half = len(cols) // 2
        folded = jnp.concatenate([sum(cols[1:half], cols[0]), sum(cols[half + 1 :], cols[half])], axis=0)
        high, low = halves(folded)
        side = lax.dot_general(
            jnp.ones((8, 256), BF16),
            jnp.concatenate([high, low], axis=1),
            (((1,), (1,)), ((), ())),
            preferred_element_type=F32,
        )[:1]
        store(k, jnp.concatenate([*top, side], axis=1))


def wide_rows(ref, start, count):
    return jnp.concatenate([ref[:, start + j, :] for j in range(count)], axis=1)


def flux_columns(corrs, kinds, lx, ly):
    nx, ny = lx // 128, ly // 128
    rows = jnp.concatenate(
        [sum(wide_rows(corr, 2 * ny + n * nx, nx)[:kinds] for corr in corrs) for n in range(2)], axis=0
    )
    rows = jnp.concatenate([rows, jnp.zeros((128 - rows.shape[0], lx), F32)], axis=0)
    return jnp.transpose(rows)


def transform_back(spec, group, corrs, columns, tabs):
    kinds, lx, ly = spec.shape
    ny = ly // 128
    spectra = []
    for k in group:
        piece = lambda start: jnp.broadcast_to(
            sum(
                jnp.concatenate([corr[k, start + j : start + j + 1, :] for j in range(ny)], axis=1)
                for corr in corrs
            ),
            (lx // 2, ly),
        )
        column = lambda at: jnp.broadcast_to(columns[:, at : at + 1], (lx, ly // 2))
        along = jnp.concatenate([piece(0), piece(ny)], axis=0)
        across = jnp.concatenate([column(k), column(kinds + k)], axis=1)
        spectra.append(spec[k] + (tabs["pull_x"][...] * along + tabs["pull_y"][...] * across))
    lines = times_left(tabs["inv_x"], jnp.concatenate(spectra, axis=1))
    lines = jnp.concatenate([lines[:, i * ly : (i + 1) * ly] for i in range(len(group))], axis=0)
    fields = lines_back(lines, tabs)
    return [fields[i * lx : (i + 1) * lx] for i in range(len(group))]


def add_rim(field, k, rim_rows, rim_cols):
    kinds, lx, ly = field.shape
    field[k, 0:1, :] += rim_rows[k : k + 1, :]
    field[k, lx - 1 : lx, :] += rim_rows[kinds + k : kinds + k + 1, :]
    row = lax.broadcasted_iota(jnp.int32, (8, 1), 0)
    at = lax.broadcasted_iota(jnp.int32, (8, 128), 1)
    for start, source, lane in ((0, k, 0), (ly - 128, kinds + k, 127)):
        cells = jnp.where(row == 0, rim_cols[source : source + 1, :], 0.0)
        where = jnp.where((row == 0) & (at == lane), 1.0, 0.0).astype(F32)
        field[k, :, start : start + 128] += outer_sum(cells, where)


def lane_sum(x):
    return jnp.sum(x, axis=0, keepdims=True)


def store_sums(pay, start, rows):
    rest = pay.shape[1] - start
    row = lax.broadcasted_iota(jnp.int32, (rest, 128), 0)
    block = jnp.zeros((rest, 128), F32)
    for j, value in enumerate(rows):
        block = jnp.where(row == j, value, block)
    for d in range(pay.shape[0]):
        pay[d, start:, :] = block


GROUP = 2
PARTS = 4
FACE = (
    "cross_e",
    "cross_o",
    "cross_te",
    "cross_to",
    "cos_x",
    "cos_xt",
    "gap_x",
    "gap_y",
    "fourier",
    "twist",
    "gather",
    "scatter",
)


def destinations(k, kinds, gx, gy):
    return [k * gy + p + kinds * gy * copy for copy in range(gx // kinds) for p in range(gy)]


def store_line(pay, places, line):
    for d in places:
        for j in range(line.shape[1] // 128):
            pay[d, j : j + 1, :] = line[:, j * 128 : (j + 1) * 128]


def edge_kernel(_, state, rows_first, rows_last, cols_first, cols_last):
    kinds, lx = cols_first.shape
    last = state.shape[3] - 1
    rows_first[...] = state[0, 0]
    rows_last[...] = state[lx - 1, 0]
    lane = lax.broadcasted_iota(jnp.int32, (kinds, 128), 1)
    for start in range(0, lx, 128):
        first_cells = jnp.zeros((kinds, 128), F32)
        last_cells = jnp.zeros((kinds, 128), F32)
        for x in range(128):
            first_cells = jnp.where(lane == x, state[start + x, 0, :, :128][:, :1], first_cells)
            last_cells = jnp.where(lane == x, state[start + x, 0, :, last - 127 :][:, 127:], last_cells)
        cols_first[:, start : start + 128] = first_cells
        cols_last[:, start : start + 128] = last_cells


def in_turn(stages, count):
    for turn in range(count + len(stages) - 1):
        for behind, stage in enumerate(stages):
            if 0 <= turn - behind < count:
                stage(turn - behind)


def start_kernel(parts, tabs, state, mob_hbm, cells, mob, r0, spec, line_out, field, lines, base, mob_sem):
    lx, kinds, ly = field.shape
    size = lx // parts
    mob_copy = pltpu.make_async_copy(mob_hbm.at[:, 0, :], mob, mob_sem.at[0])
    mob_copy.start()
    lane = lax.broadcasted_iota(jnp.int32, (kinds, ly), 1)

    def force(part):
        if part == 0:
            mob_copy.wait()
        for row in range(part * size, (part + 1) * size, 8):
            total = sum(state[row : row + 8, 0, k, :] ** 2 for k in range(kinds))
            base[row // 8] = -linear_coef + 2.0 * cross_coef * total
            rates = time_step * mob[row : row + 8, :]
            for j in range(8):
                mid = state[row + j, 0]
                around = state[max(row + j - 1, 0), 0] + state[min(row + j + 1, lx - 1), 0]
                left = jnp.where(lane == 0, mid, pltpu.roll(mid, 1, 1))
                right = jnp.where(lane == ly - 1, mid, pltpu.roll(mid, ly - 1, 1))
                lap = around + (left + right) - 4.0 * mid
                react = mid * (base[row // 8, j : j + 1, :] + (cubic_coef - 2.0 * cross_coef) * (mid * mid))
                field[row + j] = rates[j : j + 1, :] * (gradient_coef * lap - react)

    def rows_out(part):
        span = slice(part * size, (part + 1) * size)
        rows = field[span].reshape(size * kinds, ly)
        lines[span] = lines_out(rows, tabs).reshape(size, kinds, ly)
        for row in range(part * size, (part + 1) * size, 8):
            for k in range(kinds):
                cells[k, row : row + 8, :] = state[row : row + 8, 0, k, :]
                r0[k, row : row + 8, :] = field[row : row + 8, k, :]

    in_turn((force, rows_out), parts)
    for k in range(0, kinds, GROUP):
        group = list(range(k, k + GROUP))
        modes_out(
            [lines[:, g, :] for g in group], group, spec, tabs, lambda g, line: store_line(line_out, [g], line)
        )


def rim_kernel(gx, gy, lx, ly, tabs, *refs):
    line, lo, hi, near_left, near_right, own_left, own_right, st, mob, pay, corr, rows_out, cols_out = refs
    kinds = line.shape[0]
    nx, ny = lx // 128, ly // 128
    hx, hy = lx // 2, ly // 2

    def column(start, lane):
        where = jnp.where(lax.broadcasted_iota(jnp.int32, (8, 128), 1) == lane, 1.0, 0.0).astype(F32)
        return lax.dot_general(
            where,
            mob[:, start : start + 128],
            (((1,), (1,)), ((), ())),
            precision=lax.Precision.HIGHEST,
            preferred_element_type=F32,
        )

    top = stiffness * mob[0:1, :] * (lo[...] - st[:, 0, :])
    bottom = stiffness * mob[lx - 1 : lx, :] * (hi[...] - st[:, lx - 1, :])
    left = stiffness * column(0, 0) * (near_left[...] - own_left[...])
    right = stiffness * column(ly - 128, 127) * (near_right[...] - own_right[...])
    rows = jnp.concatenate([top, bottom], axis=0)
    cols = jnp.concatenate([left, right], axis=0)
    rows_out[...] = rows
    cols_out[...] = cols
    rows = lines_out(rows, tabs)
    cols = times_right(cols, tabs["cos_xt"])
    row_even, row_odd = rows[:kinds] + rows[kinds:], rows[:kinds] - rows[kinds:]
    col_even, col_odd = cols[:kinds] + cols[kinds:], cols[:kinds] - cols[kinds:]

    def spread(even, odd, table, width):
        both = times_right(jnp.concatenate([even, odd], axis=0), tabs[table])
        lane = lax.broadcasted_iota(jnp.int32, (kinds, both.shape[1]), 1)
        return jnp.where(lane < width, both[:kinds], both[kinds:])

    add = [
        tabs["self_x"][0:1, :] * row_even + spread(col_even[:, :hx], col_odd[:, :hx], "cross_e", hy),
        tabs["self_x"][1:2, :] * row_odd + spread(col_even[:, hx:], col_odd[:, hx:], "cross_o", hy),
        tabs["self_y"][0:1, :] * col_even
        + spread(row_even[:, :hy], row_odd[:, :hy], "cross_te", hx),
        tabs["self_y"][1:2, :] * col_odd
        + spread(row_even[:, hy:], row_odd[:, hy:], "cross_to", hx),
    ]
    add = jnp.concatenate(add, axis=1)
    share = jnp.concatenate([row_even, row_odd, col_even, col_odd], axis=1)
    count = 2 * (nx + ny)
    for j in range(corr.shape[1]):
        if j < count:
            corr[:, j, :] = share[:, j * 128 : (j + 1) * 128]
            value = line[:, j, :] + add[:, j * 128 : (j + 1) * 128]
        else:
            corr[:, j, :] = jnp.zeros((kinds, 128), F32)
            value = jnp.zeros((kinds, 128), F32)
        for copy in range(gx // kinds):
            for p in range(gy):
                pay[pl.ds(copy * kinds * gy + p, kinds, stride=gy), j, :] = value


def middle_kernel(gx, gy, nrow, tabs, *refs):
    corr, rim, rim_rows, rim_cols, st, mob, _, _, r0, spec, field, q1, pay, acc = refs
    kinds, lx, ly = r0.shape
    acc[...] = jnp.zeros_like(acc)
    columns = flux_columns((corr, rim), kinds, lx, ly)
    for k in range(0, kinds, GROUP):
        group = list(range(k, k + GROUP))
        for g, cells in zip(group, transform_back(spec, group, (corr, rim), columns, tabs)):
            field[g] = cells
            add_rim(r0, g, rim_rows, rim_cols)

    @pl.loop(0, lx // 8)
    def _(i):
        row = pl.multiple_of(i * 8, 8)
        for j in range(ly // 128):
            lanes = slice(j * 128, (j + 1) * 128)
            move = mob[pl.ds(row, 8), lanes]
            rate = time_step * move
            s = [st[k, pl.ds(row, 8), lanes] for k in range(kinds)]
            z = [field[k, pl.ds(row, 8), lanes] for k in range(kinds)]
            squares = [v * v for v in s]
            total = sum(squares)
            coupled = sum(a * b for a, b in zip(s, z))
            base = 1.0 - move + rate * (-linear_coef + 2.0 * cross_coef * total)
            square_coef = (3.0 * cubic_coef - 6.0 * cross_coef) * rate
            pull = (4.0 * cross_coef) * rate * coupled
            parts = [jnp.zeros((8, 128), F32)] * 2
            for k in range(kinds):
                old = r0[k, pl.ds(row, 8), lanes]
                image = z[k] * (base + square_coef * squares[k]) + pull * s[k] + move * old
                q1[k, pl.ds(row, 8), lanes] = image
                pairs = ((old, old), (old, image))
                parts = [p + a * b for p, (a, b) in zip(parts, pairs)]
            for n in range(2):
                acc[n] += parts[n]

    for k in range(0, kinds, GROUP):
        group = list(range(k, k + GROUP))
        lines = lines_out(jnp.concatenate([q1[g] for g in group], axis=0), tabs)
        modes_out(
            [lines[i * lx : (i + 1) * lx] for i in range(GROUP)],
            group,
            spec,
            tabs,
            lambda g, line: store_line(pay, destinations(g, kinds, gx, gy), line),
        )
    store_sums(pay, nrow, [lane_sum(acc[n]) for n in range(2)])


def last_kernel(nrow, tabs, corr, st, mob, spec, r0, q1, z1, field, sums, acc):
    kinds, lx, ly = r0.shape
    acc[...] = jnp.zeros_like(acc)
    height = corr[0, nrow + 1 : nrow + 2, :] / corr[0, nrow : nrow + 1, :]
    columns = flux_columns((corr,), kinds, lx, ly)
    for k in range(0, kinds, GROUP):
        group = list(range(k, k + GROUP))
        for g, cells in zip(group, transform_back(spec, group, (corr,), columns, tabs)):
            field[g] = cells - height[:, :1] * z1[g]

    @pl.loop(0, lx // 8)
    def _(i):
        row = pl.multiple_of(i * 8, 8)
        for j in range(ly // 128):
            lanes = slice(j * 128, (j + 1) * 128)
            move = mob[pl.ds(row, 8), lanes]
            rate = time_step * move
            s = [st[k, pl.ds(row, 8), lanes] for k in range(kinds)]
            z = [field[k, pl.ds(row, 8), lanes] for k in range(kinds)]
            squares = [v * v for v in s]
            total = sum(squares)
            coupled = sum(a * b for a, b in zip(s, z))
            base = 1.0 - move + rate * (-linear_coef + 2.0 * cross_coef * total)
            square_coef = (3.0 * cubic_coef - 6.0 * cross_coef) * rate
            pull = (4.0 * cross_coef) * rate * coupled
            parts = [jnp.zeros((8, 128), F32)] * 4
            for k in range(kinds):
                old = r0[k, pl.ds(row, 8), lanes]
                basis = q1[k, pl.ds(row, 8), lanes] - height * old
                image = z[k] * (base + square_coef * squares[k]) + pull * s[k] + move * basis
                pairs = ((basis, basis), (basis, image), (old, image), (image, image))
                parts = [p + a * b for p, (a, b) in zip(parts, pairs)]
            for n in range(4):
                acc[n] += parts[n]

    store_sums(sums, 0, [lane_sum(acc[n]) for n in range(4)])


def face_kernel(gx, gy, lx, ly, nrow, tabs, place, pay, out):
    nx, ny = lx // 128, ly // 128
    hx, hy = lx // 2, ly // 2
    blocks = gx * gy
    piece = functools.partial(wide_rows, pay)
    t_even, t_odd = piece(0, ny), piece(ny, ny)
    s_even, s_odd = piece(2 * ny, nx), piece(2 * ny + nx, nx)

    def turn(a, shift):
        shift = shift % a.shape[0]
        return a if shift == 0 else pltpu.roll(a, shift, 0)

    def group(a, shift):
        by = lax.broadcasted_iota(jnp.int32, a.shape, 0) % gy
        shift = shift % gy
        if shift == 0:
            return a
        return jnp.where(by < gy - shift, turn(a, -shift), turn(a, gy - shift))

    def circulant(coef, a, move, count):
        value = coef(0) * a
        for d in range(1, count // 2 + 1):
            near = move(a, d) if 2 * d == count else move(a, d) + move(a, -d)
            value = value + coef(d) * near
        return value

    def solve_x(jump, step):
        return circulant(lambda d: tabs["gap_x"][d : d + 1, :], jump, lambda a, d: turn(a, -d * step), gx)

    def spread(minus, plus, table, width):
        count = minus.shape[0]
        both = times_right(jnp.concatenate([minus, plus], axis=0), tabs[table])
        lane = lax.broadcasted_iota(jnp.int32, (count, both.shape[1]), 1)
        return jnp.where(lane < width, -both[:count], both[count:])

    flux = solve_x(t_even - t_odd - turn(t_even + t_odd, -gy), gy)
    minus, plus = flux - turn(flux, gy), flux + turn(flux, gy)
    s_even = s_even + spread(minus[:, :hy], plus[:, :hy], "cross_te", hx)
    s_odd = s_odd + spread(minus[:, hy:], plus[:, hy:], "cross_to", hx)
    jump = s_even - s_odd - group(s_even + s_odd, 1)
    lines = times_left(tabs["gather"][:, : 3 * blocks], times_right(jump, tabs["cos_x"]))
    rows = lines.shape[0] // 2
    real, imag = lines[:rows], lines[rows:]
    cosine, sine = tabs["twist"][:rows, :], tabs["twist"][rows:, :]
    turned = jnp.concatenate([real * cosine + imag * sine, imag * cosine - real * sine], axis=0)
    both = times_right(turned, tabs["fourier"])
    waves = jnp.concatenate(
        [both[:rows, :lx] + both[rows:, lx:], both[rows:, :lx] - both[:rows, lx:]], axis=0
    )
    waves = circulant(lambda d: tabs["gap_y"][2 * rows * d : 2 * rows * (d + 1), :], waves, group, gy)
    both = times_right(waves, tabs["fourier"])
    real = both[:rows, :lx] - both[rows:, lx:]
    imag = both[:rows, lx:] + both[rows:, :lx]
    turned = jnp.concatenate([real * cosine - imag * sine, real * sine + imag * cosine], axis=0)
    flow = times_right(times_left(tabs["scatter"][:, : 6 * rows], turned), tabs["cos_xt"])
    flow_minus, flow_plus = flow - group(flow, -1), flow + group(flow, -1)
    row = lax.broadcasted_iota(jnp.int32, (gx, blocks), 0)
    col = lax.broadcasted_iota(jnp.int32, (gx, blocks), 1)
    pick = jnp.concatenate([jnp.where(col == row * gy + place[0], 1.0, 0.0)] * 3, axis=1).astype(BF16)
    pool = thirds(jnp.concatenate([t_even, t_odd, flow_minus, flow_plus], axis=1))
    chosen = jnp.dot(pick, jnp.concatenate(pool, axis=0).astype(BF16), preferred_element_type=F32)
    t_even, t_odd = chosen[:, :ly], chosen[:, ly : 2 * ly]
    minus, plus = chosen[:, 2 * ly : 2 * ly + lx], chosen[:, 2 * ly + lx :]
    t_even = t_even + spread(minus[:, :hx], plus[:, :hx], "cross_e", hy)
    t_odd = t_odd + spread(minus[:, hx:], plus[:, hx:], "cross_o", hy)
    flux = solve_x(t_even - t_odd - turn(t_even + t_odd, -1), 1)
    line = jnp.concatenate([turn(flux, 1) - flux, flux + turn(flux, 1), -minus, plus], axis=1)
    for j in range(line.shape[1] // 128):
        out[:, j, :] = line[:, j * 128 : (j + 1) * 128]
    for n in range(nrow, nrow + 2):
        total = jnp.sum(jnp.sum(pay[:, n, :], axis=0, keepdims=True), axis=1, keepdims=True)
        out[:, n, :] = jnp.broadcast_to(total, (gx, 128))


def finish_kernel(nrow, _, sums, corr, st, z1, z2, out_hbm, out, sem):
    beta_sq = corr[0, nrow : nrow + 1, :]
    top_left = corr[0, nrow + 1 : nrow + 2, :] / beta_sq
    beta = jnp.sqrt(beta_sq)
    total = jnp.sum(jnp.sum(sums[...], axis=0), axis=1, keepdims=True)
    total = jnp.broadcast_to(total, (8, 128))
    length_sq, cross, first, image_sq = [total[n : n + 1, :] for n in range(4)]
    length = jnp.sqrt(length_sq)
    below_first = length / beta
    top_right = first / (beta * length)
    middle_right = cross / length_sq
    bottom_sq = image_sq / length_sq - top_right * top_right - middle_right * middle_right
    first_radius = jnp.sqrt(top_left * top_left + below_first * below_first)
    first_cosine = top_left / first_radius
    first_sine = below_first / first_radius
    upper_right = first_cosine * top_right + first_sine * middle_right
    lower_right = -first_sine * top_right + first_cosine * middle_right
    lower_target = -first_sine * beta
    second_coef = lower_right * lower_target / (lower_right * lower_right + jnp.maximum(bottom_sq, 0.0))
    first_coef = (first_cosine * beta - upper_right * second_coef) / first_radius
    a = (first_coef / beta)[:, :1]
    b = (second_coef / length)[:, :1]
    lx, kinds, ly = out.shape
    parts = sem.shape[0]
    size = lx // parts
    copies = []
    for c in range(parts):

        @pl.loop(c * size // 8, (c + 1) * size // 8)
        def _(i):
            row = pl.multiple_of(i * 8, 8)
            for k in range(kinds):
                update = a * z1[k, pl.ds(row, 8), :] + b * z2[k, pl.ds(row, 8), :]
                out[pl.ds(row, 8), k, :] = st[k, pl.ds(row, 8), :] + update

        copies.append(
            pltpu.make_async_copy(
                out.at[pl.ds(c * size, size)], out_hbm.at[pl.ds(c * size, size), 0], sem.at[c]
            )
        )
        copies[-1].start()
    for copy in copies:
        copy.wait()


def halo(rows_first, rows_last, cols_first, cols_last):
    def shift(cells, axis, step):
        count = lax.axis_size(axis)
        return lax.ppermute(cells, axis, [(i, (i + step) % count) for i in range(count)])

    return (
        shift(rows_last, "gx", 1),
        shift(rows_first, "gx", -1),
        shift(cols_last, "gy", 1),
        shift(cols_first, "gy", -1),
    )


def body(gx, gy, state, mobility):
    lx, _, kinds, ly = state.shape
    main, face = make_tables(lx, ly, gx, gy)
    tables = {**main, **face}
    packs, places = packed(tables, lx)
    packs = [jnp.asarray(pack) for pack in packs]
    nrow = (2 * lx + 2 * ly) // 128
    width = -(-(nrow + 2) // 8) * 8
    vmem = pl.BlockSpec(memory_space=pltpu.VMEM)
    hbm = pl.BlockSpec(memory_space=pl.ANY)
    smem = pl.BlockSpec(memory_space=pltpu.SMEM)
    grant = lambda mib: pltpu.CompilerParams(vmem_limit_bytes=mib * 1024 * 1024)
    array = lambda *shape: jax.ShapeDtypeStruct(shape, F32)
    whole = array(kinds, lx, ly)
    payload = array(gx * gy, width, 128)
    dma = pltpu.SemaphoreType.DMA
    place = lax.axis_index("gy").astype(jnp.int32).reshape(1)

    def kernel(function, name, inputs, keep, **options):
        count = len(inputs)

        def run(*refs):
            tabs, refs = unpacked(refs[:2], places), refs[2:]
            function(tabs, *refs[:count], *refs[count + len(keep) :])

        specs = [smem if x is place else hbm if x is mobility else vmem for x in inputs]
        specs = [vmem] * 2 + specs + [vmem] * len(keep)
        return pl.pallas_call(
            run, in_specs=specs, compiler_params=grant(GRANTS[name]), name=name, **options
        )(*packs, *inputs, *keep)

    def faces(pay, keep):
        pay = lax.all_to_all(pay, ("gx", "gy"), split_axis=0, concat_axis=0, tiled=True)
        fluxes = kernel(
            functools.partial(face_kernel, gx, gy, lx, ly, nrow),
            "faces",
            [place, pay],
            keep,
            out_shape=array(gx, width, 128),
            out_specs=vmem,
        )
        return lax.all_to_all(fluxes, "gx", split_axis=0, concat_axis=0, tiled=True)

    rows, cols = array(kinds, ly), array(kinds, lx)
    edges = pl.pallas_call(
        edge_kernel,
        out_shape=(rows, rows, cols, cols),
        in_specs=[smem, vmem],
        out_specs=(vmem,) * 4,
        compiler_params=grant(GRANTS["edges"]),
        cost_estimate=pl.CostEstimate(flops=2 * 10**10, bytes_accessed=6 * 10**7, transcendentals=0),
        name="edges",
    )(place, state)
    near = halo(*edges)

    st, mob, r0, spec, line = kernel(
        functools.partial(start_kernel, PARTS),
        "start",
        [state, mobility],
        [],
        out_shape=(whole, array(lx, ly), whole, whole, array(kinds, width, 128)),
        out_specs=(vmem,) * 5,
        scratch_shapes=[
            pltpu.VMEM((lx, kinds, ly), F32),
            pltpu.VMEM((lx, kinds, ly), F32),
            pltpu.VMEM((lx // 8, 8, ly), F32),
            dma((1,)),
        ],
        cost_estimate=pl.CostEstimate(flops=10**10, bytes_accessed=2 * 10**7, transcendentals=0),
    )
    pay, rim, rim_rows, rim_cols = kernel(
        functools.partial(rim_kernel, gx, gy, lx, ly),
        "rim",
        [line, *near, *edges[2:], st, mob],
        [r0, spec],
        out_shape=(payload, array(kinds, width, 128), array(2 * kinds, ly), array(2 * kinds, lx)),
        out_specs=(vmem,) * 4,
    )
    corr = faces(pay, [st, mob, r0, spec, rim, rim_rows, rim_cols])
    r0, spec, z1, q1, pay = kernel(
        functools.partial(middle_kernel, gx, gy, nrow),
        "middle",
        [corr, rim, rim_rows, rim_cols, st, mob, r0, spec],
        [],
        out_shape=(whole, whole, whole, whole, payload),
        out_specs=(vmem,) * 5,
        scratch_shapes=[pltpu.VMEM((2, 8, 128), F32)],
        input_output_aliases={8: 0, 9: 1},
    )
    corr = faces(pay, [st, mob, r0, spec, z1, q1])
    z2, sums = kernel(
        functools.partial(last_kernel, nrow),
        "last",
        [corr, st, mob, spec, r0, q1, z1],
        [],
        out_shape=(whole, array(gx * gy, 8, 128)),
        out_specs=(vmem,) * 2,
        scratch_shapes=[pltpu.VMEM((4, 8, 128), F32)],
    )
    sums = lax.all_to_all(sums, ("gx", "gy"), split_axis=0, concat_axis=0, tiled=True)
    return kernel(
        functools.partial(finish_kernel, nrow),
        "finish",
        [sums, corr, st, z1, z2],
        [],
        out_shape=jax.ShapeDtypeStruct(state.shape, F32),
        out_specs=hbm,
        scratch_shapes=[pltpu.VMEM((lx, kinds, ly), F32), dma((8,))],
    )


def solution(mesh):
    return jax.shard_map(
        functools.partial(body, mesh.shape["gx"], mesh.shape["gy"]),
        mesh=mesh,
        in_specs=(P("gx", None, None, "gy"), P("gx", None, "gy")),
        out_specs=P("gx", None, None, "gy"),
        check_vma=False,
    )
```

```python
import functools
import math

import jax
import jax.numpy as jnp
import numpy as np
from jax import lax
from jax.experimental import pallas as pl
from jax.experimental.pallas import tpu as pltpu
from jax.sharding import PartitionSpec as P

linear_coef = 1.0
cubic_coef = 1.0
cross_coef = 1.5
gradient_coef = 200.0
time_step = 200.0
stiffness = time_step * gradient_coef

F32 = jnp.float32
BF16 = jnp.bfloat16
GRANTS = dict(edges=4, start=16, rim=4, faces=4, middle=14, last=14, finish=6)


def cosine_table(size):
    modes = np.arange(size)[:, None]
    cells = np.arange(size)[None, :]
    table = np.sqrt(2.0 / size) * np.cos(np.pi * modes * (cells + 0.5) / size)
    table[0] = np.sqrt(1.0 / size)
    values = 4.0 * np.sin(np.pi * np.arange(size) / (2 * size)) ** 2
    order = np.concatenate([np.arange(0, size, 2), np.arange(1, size, 2)])
    return table[order], values[order]


def split_const(table):
    high = table.astype(np.float32).astype(jnp.bfloat16)
    low = (table - high.astype(np.float64)).astype(np.float32).astype(jnp.bfloat16)
    return high, low


def right_const(table):
    high, low = split_const(table)
    return np.concatenate([high, low, high], axis=0)


def left_const(table):
    high, low = split_const(table)
    return np.concatenate([high, low, high], axis=1)


def make_tables(lx, ly, gx, gy):
    cos_x, value_x = cosine_table(lx)
    cos_y, value_y = cosine_table(ly)
    edge_x, edge_y = cos_x[:, 0], cos_y[:, 0]
    inverse = 1.0 / (1.0 + stiffness * (value_x[:, None] + value_y[None, :]))
    cross = edge_x[:, None] * edge_y[None, :] * inverse
    sign_x = np.where(np.arange(lx) < lx // 2, 1.0, -1.0)
    sign_y = np.where(np.arange(ly) < ly // 2, 1.0, -1.0)
    own = (edge_x[:, None] ** 2 * inverse).sum(0)
    other = (sign_x[:, None] * edge_x[:, None] ** 2 * inverse).sum(0)
    wave = np.arange(gx)
    eigen = 1.0 / stiffness + 2.0 * own[None] - 2.0 * other[None] * np.cos(2 * np.pi * wave / gx)[:, None]
    gap_x = np.stack(
        [(np.cos(2 * np.pi * wave * d / gx)[:, None] / eigen).mean(0) for d in range(gx // 2 + 1)]
    )
    total = lx * gx
    half = gx // 2 + 1
    rows = -(-half * gy // 8) * 8
    freq = gx * np.arange(lx)[None, :] + np.arange(half)[:, None]
    symbol = 1.0 + stiffness * (4.0 * np.sin(np.pi * freq / total) ** 2)[:, :, None] + stiffness * value_y
    own = (edge_y**2 / symbol).sum(-1)
    other = (sign_y * edge_y**2 / symbol).sum(-1)
    wave = np.arange(gy)
    eigen = 1.0 / stiffness + 2.0 * own[None] - 2.0 * other[None] * np.cos(2 * np.pi * wave / gy)[:, None, None]
    gap_y = np.zeros((gy // 2 + 1, 2 * rows, lx))
    for d in range(gy // 2 + 1):
        coef = (np.cos(2 * np.pi * wave * d / gy)[:, None, None] / eigen).mean(0)
        coef = np.repeat(coef, gy, axis=0)
        gap_y[d, : half * gy] = coef
        gap_y[d, rows : rows + half * gy] = coef
    cells = np.arange(lx)
    angle = 2 * np.pi * np.outer(cells, cells) / lx
    fourier = np.concatenate([np.cos(angle), np.sin(angle)], axis=1)
    twist = np.zeros((2, rows, lx))
    gather = np.zeros((2 * rows, gx * gy))
    scatter = np.zeros((gx * gy, 2 * rows))
    for q in range(half):
        theta = 2 * np.pi * q * cells / total
        weight = (1.0 if q in (0, gx // 2) else 2.0) / total
        for j in range(gy):
            twist[0, q * gy + j] = np.cos(theta)
            twist[1, q * gy + j] = np.sin(theta)
            for i in range(gx):
                phase = 2 * np.pi * q * i / gx
                gather[q * gy + j, i * gy + j] = np.cos(phase)
                gather[rows + q * gy + j, i * gy + j] = -np.sin(phase)
                scatter[i * gy + j, q * gy + j] = weight * np.cos(phase)
                scatter[i * gy + j, rows + q * gy + j] = -weight * np.sin(phase)
    single = lambda a: np.ascontiguousarray(a, dtype=np.float32)
    main = dict(
        fwd_ye=right_const(cos_y[: ly // 2, : ly // 2].T),
        fwd_yo=right_const(cos_y[ly // 2 :, : ly // 2].T),
        fwd_x=left_const(cos_x),
        inv_ye=right_const((cos_y / edge_y[:, None])[: ly // 2, : ly // 2]),
        inv_yo=right_const((cos_y / edge_y[:, None])[ly // 2 :, : ly // 2]),
        inv_x=left_const(cos_x.T / edge_x),
        cross=single(cross),
        over_x=single(np.tile(1.0 / edge_x, (8, 2))),
        over_y=single(np.tile(1.0 / edge_y, (8, 1))),
        pull_x=single(cross * edge_x[:, None]),
        pull_y=single(cross * edge_y[None, :]),
    )
    face = dict(
        cross_e=right_const(cross[: lx // 2]),
        cross_o=right_const(cross[lx // 2 :]),
        cross_te=right_const(cross.T[: ly // 2]),
        cross_to=right_const(cross.T[ly // 2 :]),
        cos_x=right_const(cos_x),
        cos_xt=right_const(cos_x.T),
        gap_x=single(gap_x),
        gap_y=single(gap_y.reshape(-1, lx)),
        fourier=right_const(fourier),
        twist=single(twist.reshape(-1, lx)),
        gather=left_const(gather),
        scatter=left_const(scatter),
        self_x=single(np.stack([(edge_x[:, None] ** 2 * inverse)[h].sum(0) for h in np.split(np.arange(lx), 2)])),
        self_y=single(np.stack([(edge_y**2 * inverse)[:, h].sum(1) for h in np.split(np.arange(ly), 2)])),
    )
    return main, face


def packed(tables, strip):
    arrays, places = [], []
    for kind, step in ((np.dtype(jnp.bfloat16), 16), (np.dtype(np.float32), 8)):
        strips, start = [], 0
        for name, table in tables.items():
            if table.dtype != kind:
                continue
            rows, cols = -(-table.shape[0] // step) * step, -(-table.shape[1] // strip) * strip
            wide = np.zeros((rows, cols), kind)
            wide[: table.shape[0], : table.shape[1]] = table
            for j in range(0, cols, strip):
                strips.append(wide[:, j : j + strip])
                places.append((name, len(arrays), start, *table.shape))
                start += rows
        arrays.append(np.concatenate(strips, axis=0))
    return arrays, places


class Table:
    def __init__(self, ref, starts, rows, cols):
        self.ref, self.starts, self.shape = ref, starts, (rows, cols)

    def __getitem__(self, index):
        index = (slice(None), slice(None)) if index is Ellipsis else index
        (top, bottom, _), (left, right, _) = [part.indices(size) for part, size in zip(index, self.shape)]
        strip = self.ref.shape[1]
        pieces = []
        for j, start in enumerate(self.starts):
            low, high = max(left - j * strip, 0), min(right - j * strip, strip)
            if low < high:
                pieces.append(self.ref[start + top : start + bottom, low:high])
        return pieces[0] if len(pieces) == 1 else jnp.concatenate(pieces, axis=1)


def unpacked(refs, places):
    starts, found = {}, {}
    for name, which, start, rows, cols in places:
        starts.setdefault(name, []).append(start)
        found[name] = Table(refs[which], starts[name], rows, cols)
    return found


def halves(x):
    high = x.astype(BF16)
    low = (x - high.astype(F32)).astype(BF16)
    return high, low


def times_right(x, const):
    high, low = halves(x)
    return jnp.dot(jnp.concatenate([high, high, low], axis=1), const[...], preferred_element_type=F32)


def times_left(const, x):
    high, low = halves(x)
    return jnp.dot(const[...], jnp.concatenate([high, high, low], axis=0), preferred_element_type=F32)


def thirds(x):
    high = x.astype(BF16).astype(F32)
    rest = x - high
    mid = rest.astype(BF16).astype(F32)
    return high, mid, rest - mid


def outer_sum(a, b):
    ah, am, al = thirds(a)
    bh, bm, bl = thirds(b)
    left = jnp.concatenate([ah, ah, am, am, ah, al], axis=0).astype(BF16)
    right = jnp.concatenate([bh, bm, bh, bm, bl, bh], axis=0).astype(BF16)
    return lax.dot_general(left, right, (((0,), (0,)), ((), ())), preferred_element_type=F32)


def flipped(x):
    place = 127 - lax.broadcasted_iota(jnp.int32, (x.shape[0], 128), 1)
    tiles = [x[:, j * 128 : (j + 1) * 128] for j in range(x.shape[1] // 128)]
    return jnp.concatenate(
        [jnp.take_along_axis(tile, place, axis=1, mode="promise_in_bounds") for tile in tiles[::-1]], axis=1
    )


def lines_out(x, tabs):
    half = x.shape[1] // 2
    left, right = x[:, :half], flipped(x[:, half:])
    return jnp.concatenate(
        [times_right(left + right, tabs["fwd_ye"]), times_right(left - right, tabs["fwd_yo"])], axis=1
    )


def lines_back(x, tabs):
    half = x.shape[1] // 2
    even = times_right(x[:, :half], tabs["inv_ye"])
    odd = times_right(x[:, half:], tabs["inv_yo"])
    return jnp.concatenate([even + odd, flipped(even - odd)], axis=1)


def modes_out(lines, group, spec, tabs, store):
    lx, ly = spec.shape[1:]
    hat = times_left(tabs["fwd_x"], jnp.concatenate(lines, axis=1))
    for i, k in enumerate(group):
        spectrum = hat[:, i * ly : (i + 1) * ly] * tabs["cross"][...]
        spec[k] = spectrum
        top = [jnp.sum(half, axis=0, keepdims=True) * tabs["over_y"][:1, :] for half in (spectrum[: lx // 2], spectrum[lx // 2 :])]
        cols = [spectrum[:, j * 128 : (j + 1) * 128] for j in range(ly // 128)]
        half = len(cols) // 2
        folded = jnp.concatenate([sum(cols[1:half], cols[0]), sum(cols[half + 1 :], cols[half])], axis=0)
        high, low = halves(folded)
        side = lax.dot_general(
            jnp.ones((8, 256), BF16),
            jnp.concatenate([high, low], axis=1),
            (((1,), (1,)), ((), ())),
            preferred_element_type=F32,
        )[:1]
        side = side * tabs["over_x"][:1, :]
        store(k, jnp.concatenate([*top, side], axis=1))


def wide_rows(ref, start, count):
    return jnp.concatenate([ref[:, start + j, :] for j in range(count)], axis=1)


def flux_columns(corrs, kinds, lx, ly):
    nx, ny = lx // 128, ly // 128
    rows = jnp.concatenate(
        [sum(wide_rows(corr, 2 * ny + n * nx, nx)[:kinds] for corr in corrs) for n in range(2)], axis=0
    )
    rows = jnp.concatenate([rows, jnp.zeros((128 - rows.shape[0], lx), F32)], axis=0)
    return jnp.transpose(rows)


def transform_back(spec, group, corrs, columns, tabs):
    kinds, lx, ly = spec.shape
    ny = ly // 128
    spectra = []
    for k in group:
        piece = lambda start: jnp.broadcast_to(
            sum(
                jnp.concatenate([corr[k, start + j : start + j + 1, :] for j in range(ny)], axis=1)
                for corr in corrs
            ),
            (lx // 2, ly),
        )
        column = lambda at: jnp.broadcast_to(columns[:, at : at + 1], (lx, ly // 2))
        along = jnp.concatenate([piece(0), piece(ny)], axis=0)
        across = jnp.concatenate([column(k), column(kinds + k)], axis=1)
        spectra.append(spec[k] + (tabs["pull_x"][...] * along + tabs["pull_y"][...] * across))
    lines = times_left(tabs["inv_x"], jnp.concatenate(spectra, axis=1))
    lines = jnp.concatenate([lines[:, i * ly : (i + 1) * ly] for i in range(len(group))], axis=0)
    fields = lines_back(lines, tabs)
    return [fields[i * lx : (i + 1) * lx] for i in range(len(group))]


def add_rim(field, k, rim_rows, rim_cols):
    kinds, lx, ly = field.shape
    field[k, 0:1, :] += rim_rows[k : k + 1, :]
    field[k, lx - 1 : lx, :] += rim_rows[kinds + k : kinds + k + 1, :]
    row = lax.broadcasted_iota(jnp.int32, (8, 1), 0)
    at = lax.broadcasted_iota(jnp.int32, (8, 128), 1)
    for start, source, lane in ((0, k, 0), (ly - 128, kinds + k, 127)):
        cells = jnp.where(row == 0, rim_cols[source : source + 1, :], 0.0)
        where = jnp.where((row == 0) & (at == lane), 1.0, 0.0).astype(F32)
        field[k, :, start : start + 128] += outer_sum(cells, where)


def lane_sum(x):
    return jnp.sum(x, axis=0, keepdims=True)


def store_sums(pay, start, rows):
    rest = pay.shape[1] - start
    row = lax.broadcasted_iota(jnp.int32, (rest, 128), 0)
    block = jnp.zeros((rest, 128), F32)
    for j, value in enumerate(rows):
        block = jnp.where(row == j, value, block)
    for d in range(pay.shape[0]):
        pay[d, start:, :] = block


GROUP = 4
PARTS = 4
FACE = (
    "cross_e",
    "cross_o",
    "cross_te",
    "cross_to",
    "cos_x",
    "cos_xt",
    "gap_x",
    "gap_y",
    "fourier",
    "twist",
    "gather",
    "scatter",
)


def destinations(k, kinds, gx, gy):
    return [k * gy + p + kinds * gy * copy for copy in range(gx // kinds) for p in range(gy)]


def store_line(pay, places, line):
    for d in places:
        for j in range(line.shape[1] // 128):
            pay[d, j : j + 1, :] = line[:, j * 128 : (j + 1) * 128]


def edge_kernel(_, state, rows_first, rows_last, cols_first, cols_last):
    kinds, lx = cols_first.shape
    last = state.shape[3] - 1
    rows_first[...] = state[0, 0]
    rows_last[...] = state[lx - 1, 0]
    lane = lax.broadcasted_iota(jnp.int32, (kinds, 128), 1)
    for start in range(0, lx, 128):
        first_cells = jnp.zeros((kinds, 128), F32)
        last_cells = jnp.zeros((kinds, 128), F32)
        for x in range(128):
            first_cells = jnp.where(lane == x, state[start + x, 0, :, :128][:, :1], first_cells)
            last_cells = jnp.where(lane == x, state[start + x, 0, :, last - 127 :][:, 127:], last_cells)
        cols_first[:, start : start + 128] = first_cells
        cols_last[:, start : start + 128] = last_cells


def in_turn(stages, count):
    for turn in range(count + len(stages) - 1):
        for behind, stage in enumerate(stages):
            if 0 <= turn - behind < count:
                stage(turn - behind)


def start_kernel(parts, tabs, state, mob_hbm, cells, mob, r0, spec, line_out, field, lines, base, mob_sem):
    lx, kinds, ly = field.shape
    size = lx // parts
    mob_copy = pltpu.make_async_copy(mob_hbm.at[:, 0, :], mob, mob_sem.at[0])
    mob_copy.start()
    lane = lax.broadcasted_iota(jnp.int32, (kinds, ly), 1)

    def force(part):
        if part == 0:
            mob_copy.wait()
        for row in range(part * size, (part + 1) * size, 8):
            total = sum(state[row : row + 8, 0, k, :] ** 2 for k in range(kinds))
            base[row // 8] = -linear_coef + 2.0 * cross_coef * total
            rates = time_step * mob[row : row + 8, :]
            for j in range(8):
                mid = state[row + j, 0]
                around = state[max(row + j - 1, 0), 0] + state[min(row + j + 1, lx - 1), 0]
                left = jnp.where(lane == 0, mid, pltpu.roll(mid, 1, 1))
                right = jnp.where(lane == ly - 1, mid, pltpu.roll(mid, ly - 1, 1))
                lap = around + (left + right) - 4.0 * mid
                react = mid * (base[row // 8, j : j + 1, :] + (cubic_coef - 2.0 * cross_coef) * (mid * mid))
                field[row + j] = rates[j : j + 1, :] * (gradient_coef * lap - react)

    def rows_out(part):
        span = slice(part * size, (part + 1) * size)
        rows = field[span].reshape(size * kinds, ly)
        lines[span] = lines_out(rows, tabs).reshape(size, kinds, ly)
        for row in range(part * size, (part + 1) * size, 8):
            for k in range(kinds):
                cells[k, row : row + 8, :] = state[row : row + 8, 0, k, :]
                r0[k, row : row + 8, :] = field[row : row + 8, k, :]

    in_turn((force, rows_out), parts)
    for k in range(0, kinds, GROUP):
        group = list(range(k, k + GROUP))
        modes_out(
            [lines[:, g, :] for g in group], group, spec, tabs, lambda g, line: store_line(line_out, [g], line)
        )


def rim_kernel(gx, gy, lx, ly, tabs, *refs):
    line, lo, hi, near_left, near_right, own_left, own_right, st, mob, pay, corr, rows_out, cols_out = refs
    kinds = line.shape[0]
    nx, ny = lx // 128, ly // 128
    hx, hy = lx // 2, ly // 2

    def column(start, lane):
        where = jnp.where(lax.broadcasted_iota(jnp.int32, (8, 128), 1) == lane, 1.0, 0.0).astype(F32)
        return lax.dot_general(
            where,
            mob[:, start : start + 128],
            (((1,), (1,)), ((), ())),
            precision=lax.Precision.HIGHEST,
            preferred_element_type=F32,
        )

    top = stiffness * mob[0:1, :] * (lo[...] - st[:, 0, :])
    bottom = stiffness * mob[lx - 1 : lx, :] * (hi[...] - st[:, lx - 1, :])
    left = stiffness * column(0, 0) * (near_left[...] - own_left[...])
    right = stiffness * column(ly - 128, 127) * (near_right[...] - own_right[...])
    rows = jnp.concatenate([top, bottom], axis=0)
    cols = jnp.concatenate([left, right], axis=0)
    rows_out[...] = rows
    cols_out[...] = cols
    rows = lines_out(rows, tabs)
    cols = times_right(cols, tabs["cos_xt"])
    row_even, row_odd = rows[:kinds] + rows[kinds:], rows[:kinds] - rows[kinds:]
    col_even, col_odd = cols[:kinds] + cols[kinds:], cols[:kinds] - cols[kinds:]

    def spread(even, odd, table, width):
        both = times_right(jnp.concatenate([even, odd], axis=0), tabs[table])
        lane = lax.broadcasted_iota(jnp.int32, (kinds, both.shape[1]), 1)
        return jnp.where(lane < width, both[:kinds], both[kinds:])

    add = [
        tabs["self_x"][0:1, :] * row_even + spread(col_even[:, :hx], col_odd[:, :hx], "cross_e", hy),
        tabs["self_x"][1:2, :] * row_odd + spread(col_even[:, hx:], col_odd[:, hx:], "cross_o", hy),
        tabs["self_y"][0:1, :] * col_even
        + spread(row_even[:, :hy], row_odd[:, :hy], "cross_te", hx),
        tabs["self_y"][1:2, :] * col_odd
        + spread(row_even[:, hy:], row_odd[:, hy:], "cross_to", hx),
    ]
    add = jnp.concatenate(add, axis=1)
    share = jnp.concatenate([row_even, row_odd, col_even, col_odd], axis=1)
    count = 2 * (nx + ny)
    for j in range(corr.shape[1]):
        if j < count:
            corr[:, j, :] = share[:, j * 128 : (j + 1) * 128]
            value = line[:, j, :] + add[:, j * 128 : (j + 1) * 128]
        else:
            corr[:, j, :] = jnp.zeros((kinds, 128), F32)
            value = jnp.zeros((kinds, 128), F32)
        for copy in range(gx // kinds):
            for p in range(gy):
                pay[pl.ds(copy * kinds * gy + p, kinds, stride=gy), j, :] = value


def middle_kernel(gx, gy, nrow, tabs, *refs):
    corr, rim, rim_rows, rim_cols, st, mob, _, _, r0, spec, field, q1, pay, acc = refs
    kinds, lx, ly = r0.shape
    acc[...] = jnp.zeros_like(acc)
    columns = flux_columns((corr, rim), kinds, lx, ly)
    for k in range(0, kinds, GROUP):
        group = list(range(k, k + GROUP))
        for g, cells in zip(group, transform_back(spec, group, (corr, rim), columns, tabs)):
            field[g] = cells
            add_rim(r0, g, rim_rows, rim_cols)

    @pl.loop(0, lx // 8, unroll=4)
    def _(i):
        row = pl.multiple_of(i * 8, 8)
        for j in range(ly // 128):
            lanes = slice(j * 128, (j + 1) * 128)
            move = mob[pl.ds(row, 8), lanes]
            rate = time_step * move
            s = [st[k, pl.ds(row, 8), lanes] for k in range(kinds)]
            z = [field[k, pl.ds(row, 8), lanes] for k in range(kinds)]
            squares = [v * v for v in s]
            total = sum(squares)
            coupled = sum(a * b for a, b in zip(s, z))
            base = 1.0 - move + rate * (-linear_coef + 2.0 * cross_coef * total)
            square_coef = (3.0 * cubic_coef - 6.0 * cross_coef) * rate
            pull = (4.0 * cross_coef) * rate * coupled
            parts = [jnp.zeros((8, 128), F32)] * 2
            for k in range(kinds):
                old = r0[k, pl.ds(row, 8), lanes]
                image = z[k] * (base + square_coef * squares[k]) + pull * s[k] + move * old
                q1[k, pl.ds(row, 8), lanes] = image
                pairs = ((old, old), (old, image))
                parts = [p + a * b for p, (a, b) in zip(parts, pairs)]
            for n in range(2):
                acc[n] += parts[n]

    for k in range(0, kinds, GROUP):
        group = list(range(k, k + GROUP))
        lines = lines_out(jnp.concatenate([q1[g] for g in group], axis=0), tabs)
        modes_out(
            [lines[i * lx : (i + 1) * lx] for i in range(GROUP)],
            group,
            spec,
            tabs,
            lambda g, line: store_line(pay, destinations(g, kinds, gx, gy), line),
        )
    store_sums(pay, nrow, [lane_sum(acc[n]) for n in range(2)])


def last_kernel(nrow, tabs, corr, st, mob, spec, r0, q1, z1, field, sums, acc):
    kinds, lx, ly = r0.shape
    acc[...] = jnp.zeros_like(acc)
    height = corr[0, nrow + 1 : nrow + 2, :] / corr[0, nrow : nrow + 1, :]
    columns = flux_columns((corr,), kinds, lx, ly)
    for k in range(0, kinds, GROUP):
        group = list(range(k, k + GROUP))
        for g, cells in zip(group, transform_back(spec, group, (corr,), columns, tabs)):
            field[g] = cells - height[:, :1] * z1[g]

    @pl.loop(0, lx // 8, unroll=4)
    def _(i):
        row = pl.multiple_of(i * 8, 8)
        for j in range(ly // 128):
            lanes = slice(j * 128, (j + 1) * 128)
            move = mob[pl.ds(row, 8), lanes]
            rate = time_step * move
            s = [st[k, pl.ds(row, 8), lanes] for k in range(kinds)]
            z = [field[k, pl.ds(row, 8), lanes] for k in range(kinds)]
            squares = [v * v for v in s]
            total = sum(squares)
            coupled = sum(a * b for a, b in zip(s, z))
            base = 1.0 - move + rate * (-linear_coef + 2.0 * cross_coef * total)
            square_coef = (3.0 * cubic_coef - 6.0 * cross_coef) * rate
            pull = (4.0 * cross_coef) * rate * coupled
            parts = [jnp.zeros((8, 128), F32)] * 4
            for k in range(kinds):
                old = r0[k, pl.ds(row, 8), lanes]
                basis = q1[k, pl.ds(row, 8), lanes] - height * old
                image = z[k] * (base + square_coef * squares[k]) + pull * s[k] + move * basis
                pairs = ((basis, basis), (basis, image), (old, image), (image, image))
                parts = [p + a * b for p, (a, b) in zip(parts, pairs)]
            for n in range(4):
                acc[n] += parts[n]

    store_sums(sums, 0, [lane_sum(acc[n]) for n in range(4)])


def face_kernel(gx, gy, lx, ly, nrow, tabs, place, pay, out):
    nx, ny = lx // 128, ly // 128
    hx, hy = lx // 2, ly // 2
    blocks = gx * gy
    piece = functools.partial(wide_rows, pay)
    t_even, t_odd = piece(0, ny), piece(ny, ny)
    s_even, s_odd = piece(2 * ny, nx), piece(2 * ny + nx, nx)

    def turn(a, shift):
        shift = shift % a.shape[0]
        return a if shift == 0 else pltpu.roll(a, shift, 0)

    def group(a, shift):
        by = lax.broadcasted_iota(jnp.int32, a.shape, 0) % gy
        shift = shift % gy
        if shift == 0:
            return a
        return jnp.where(by < gy - shift, turn(a, -shift), turn(a, gy - shift))

    def circulant(coef, a, move, count):
        value = coef(0) * a
        for d in range(1, count // 2 + 1):
            near = move(a, d) if 2 * d == count else move(a, d) + move(a, -d)
            value = value + coef(d) * near
        return value

    def solve_x(jump, step):
        return circulant(lambda d: tabs["gap_x"][d : d + 1, :], jump, lambda a, d: turn(a, -d * step), gx)

    def spread(minus, plus, table, width):
        count = minus.shape[0]
        both = times_right(jnp.concatenate([minus, plus], axis=0), tabs[table])
        lane = lax.broadcasted_iota(jnp.int32, (count, both.shape[1]), 1)
        return jnp.where(lane < width, -both[:count], both[count:])

    flux = solve_x(t_even - t_odd - turn(t_even + t_odd, -gy), gy)
    minus, plus = flux - turn(flux, gy), flux + turn(flux, gy)
    s_even = s_even + spread(minus[:, :hy], plus[:, :hy], "cross_te", hx)
    s_odd = s_odd + spread(minus[:, hy:], plus[:, hy:], "cross_to", hx)
    jump = s_even - s_odd - group(s_even + s_odd, 1)
    lines = times_left(tabs["gather"][:, : 3 * blocks], times_right(jump, tabs["cos_x"]))
    rows = lines.shape[0] // 2
    real, imag = lines[:rows], lines[rows:]
    cosine, sine = tabs["twist"][:rows, :], tabs["twist"][rows:, :]
    turned = jnp.concatenate([real * cosine + imag * sine, imag * cosine - real * sine], axis=0)
    both = times_right(turned, tabs["fourier"])
    waves = jnp.concatenate(
        [both[:rows, :lx] + both[rows:, lx:], both[rows:, :lx] - both[:rows, lx:]], axis=0
    )
    waves = circulant(lambda d: tabs["gap_y"][2 * rows * d : 2 * rows * (d + 1), :], waves, group, gy)
    both = times_right(waves, tabs["fourier"])
    real = both[:rows, :lx] - both[rows:, lx:]
    imag = both[:rows, lx:] + both[rows:, :lx]
    turned = jnp.concatenate([real * cosine - imag * sine, real * sine + imag * cosine], axis=0)
    flow = times_right(times_left(tabs["scatter"][:, : 6 * rows], turned), tabs["cos_xt"])
    flow_minus, flow_plus = flow - group(flow, -1), flow + group(flow, -1)
    row = lax.broadcasted_iota(jnp.int32, (gx, blocks), 0)
    col = lax.broadcasted_iota(jnp.int32, (gx, blocks), 1)
    pick = jnp.concatenate([jnp.where(col == row * gy + place[0], 1.0, 0.0)] * 3, axis=1).astype(BF16)
    pool = thirds(jnp.concatenate([t_even, t_odd, flow_minus, flow_plus], axis=1))
    chosen = jnp.dot(pick, jnp.concatenate(pool, axis=0).astype(BF16), preferred_element_type=F32)
    t_even, t_odd = chosen[:, :ly], chosen[:, ly : 2 * ly]
    minus, plus = chosen[:, 2 * ly : 2 * ly + lx], chosen[:, 2 * ly + lx :]
    t_even = t_even + spread(minus[:, :hx], plus[:, :hx], "cross_e", hy)
    t_odd = t_odd + spread(minus[:, hx:], plus[:, hx:], "cross_o", hy)
    flux = solve_x(t_even - t_odd - turn(t_even + t_odd, -1), 1)
    line = jnp.concatenate([turn(flux, 1) - flux, flux + turn(flux, 1), -minus, plus], axis=1)
    for j in range(line.shape[1] // 128):
        out[:, j, :] = line[:, j * 128 : (j + 1) * 128]
    for n in range(nrow, nrow + 2):
        total = jnp.sum(jnp.sum(pay[:, n, :], axis=0, keepdims=True), axis=1, keepdims=True)
        out[:, n, :] = jnp.broadcast_to(total, (gx, 128))


def finish_kernel(nrow, _, sums, corr, st, z1, z2, out_hbm, out, sem):
    beta_sq = corr[0, nrow : nrow + 1, :]
    top_left = corr[0, nrow + 1 : nrow + 2, :] / beta_sq
    beta = jnp.sqrt(beta_sq)
    total = jnp.sum(jnp.sum(sums[...], axis=0), axis=1, keepdims=True)
    total = jnp.broadcast_to(total, (8, 128))
    length_sq, cross, first, image_sq = [total[n : n + 1, :] for n in range(4)]
    length = jnp.sqrt(length_sq)
    below_first = length / beta
    top_right = first / (beta * length)
    middle_right = cross / length_sq
    bottom_sq = image_sq / length_sq - top_right * top_right - middle_right * middle_right
    first_radius = jnp.sqrt(top_left * top_left + below_first * below_first)
    first_cosine = top_left / first_radius
    first_sine = below_first / first_radius
    upper_right = first_cosine * top_right + first_sine * middle_right
    lower_right = -first_sine * top_right + first_cosine * middle_right
    lower_target = -first_sine * beta
    second_coef = lower_right * lower_target / (lower_right * lower_right + jnp.maximum(bottom_sq, 0.0))
    first_coef = (first_cosine * beta - upper_right * second_coef) / first_radius
    a = (first_coef / beta)[:, :1]
    b = (second_coef / length)[:, :1]
    lx, kinds, ly = out.shape
    parts = sem.shape[0]
    size = lx // parts
    copies = []
    for c in range(parts):

        @pl.loop(c * size // 8, (c + 1) * size // 8)
        def _(i):
            row = pl.multiple_of(i * 8, 8)
            for k in range(kinds):
                update = a * z1[k, pl.ds(row, 8), :] + b * z2[k, pl.ds(row, 8), :]
                out[pl.ds(row, 8), k, :] = st[k, pl.ds(row, 8), :] + update

        copies.append(
            pltpu.make_async_copy(
                out.at[pl.ds(c * size, size)], out_hbm.at[pl.ds(c * size, size), 0], sem.at[c]
            )
        )
        copies[-1].start()
    for copy in copies:
        copy.wait()


def halo(rows_first, rows_last, cols_first, cols_last):
    def shift(cells, axis, step):
        count = lax.axis_size(axis)
        return lax.ppermute(cells, axis, [(i, (i + step) % count) for i in range(count)])

    return (
        shift(rows_last, "gx", 1),
        shift(rows_first, "gx", -1),
        shift(cols_last, "gy", 1),
        shift(cols_first, "gy", -1),
    )


def body(gx, gy, state, mobility):
    lx, _, kinds, ly = state.shape
    main, face = make_tables(lx, ly, gx, gy)
    tables = {**main, **face}
    packs, places = packed(tables, lx)
    packs = [jnp.asarray(pack) for pack in packs]
    nrow = (2 * lx + 2 * ly) // 128
    width = -(-(nrow + 2) // 8) * 8
    vmem = pl.BlockSpec(memory_space=pltpu.VMEM)
    hbm = pl.BlockSpec(memory_space=pl.ANY)
    smem = pl.BlockSpec(memory_space=pltpu.SMEM)
    grant = lambda mib: pltpu.CompilerParams(vmem_limit_bytes=mib * 1024 * 1024)
    array = lambda *shape: jax.ShapeDtypeStruct(shape, F32)
    whole = array(kinds, lx, ly)
    payload = array(gx * gy, width, 128)
    dma = pltpu.SemaphoreType.DMA
    place = lax.axis_index("gy").astype(jnp.int32).reshape(1)

    def kernel(function, name, inputs, keep, **options):
        count = len(inputs)

        def run(*refs):
            tabs, refs = unpacked(refs[:2], places), refs[2:]
            function(tabs, *refs[:count], *refs[count + len(keep) :])

        specs = [smem if x is place else hbm if x is mobility else vmem for x in inputs]
        specs = [vmem] * 2 + specs + [vmem] * len(keep)
        return pl.pallas_call(
            run, in_specs=specs, compiler_params=grant(GRANTS[name]), name=name, **options
        )(*packs, *inputs, *keep)

    def faces(pay, keep):
        pay = lax.all_to_all(pay, ("gx", "gy"), split_axis=0, concat_axis=0, tiled=True)
        fluxes = kernel(
            functools.partial(face_kernel, gx, gy, lx, ly, nrow),
            "faces",
            [place, pay],
            keep,
            out_shape=array(gx, width, 128),
            out_specs=vmem,
        )
        return lax.all_to_all(fluxes, "gx", split_axis=0, concat_axis=0, tiled=True)

    rows, cols = array(kinds, ly), array(kinds, lx)
    edges = pl.pallas_call(
        edge_kernel,
        out_shape=(rows, rows, cols, cols),
        in_specs=[smem, vmem],
        out_specs=(vmem,) * 4,
        compiler_params=grant(GRANTS["edges"]),
        cost_estimate=pl.CostEstimate(flops=2 * 10**10, bytes_accessed=6 * 10**7, transcendentals=0),
        name="edges",
    )(place, state)
    near = halo(*edges)

    st, mob, r0, spec, line = kernel(
        functools.partial(start_kernel, PARTS),
        "start",
        [state, mobility],
        [],
        out_shape=(whole, array(lx, ly), whole, whole, array(kinds, width, 128)),
        out_specs=(vmem,) * 5,
        scratch_shapes=[
            pltpu.VMEM((lx, kinds, ly), F32),
            pltpu.VMEM((lx, kinds, ly), F32),
            pltpu.VMEM((lx // 8, 8, ly), F32),
            dma((1,)),
        ],
        cost_estimate=pl.CostEstimate(flops=10**10, bytes_accessed=2 * 10**7, transcendentals=0),
    )
    pay, rim, rim_rows, rim_cols = kernel(
        functools.partial(rim_kernel, gx, gy, lx, ly),
        "rim",
        [line, *near, *edges[2:], st, mob],
        [r0, spec],
        out_shape=(payload, array(kinds, width, 128), array(2 * kinds, ly), array(2 * kinds, lx)),
        out_specs=(vmem,) * 4,
    )
    corr = faces(pay, [st, mob, r0, spec, rim, rim_rows, rim_cols])
    r0, spec, z1, q1, pay = kernel(
        functools.partial(middle_kernel, gx, gy, nrow),
        "middle",
        [corr, rim, rim_rows, rim_cols, st, mob, r0, spec],
        [],
        out_shape=(whole, whole, whole, whole, payload),
        out_specs=(vmem,) * 5,
        scratch_shapes=[pltpu.VMEM((2, 8, 128), F32)],
        input_output_aliases={8: 0, 9: 1},
    )
    corr = faces(pay, [st, mob, r0, spec, z1, q1])
    z2, sums = kernel(
        functools.partial(last_kernel, nrow),
        "last",
        [corr, st, mob, spec, r0, q1, z1],
        [],
        out_shape=(whole, array(gx * gy, 8, 128)),
        out_specs=(vmem,) * 2,
        scratch_shapes=[pltpu.VMEM((4, 8, 128), F32)],
    )
    sums = lax.all_to_all(sums, ("gx", "gy"), split_axis=0, concat_axis=0, tiled=True)
    return kernel(
        functools.partial(finish_kernel, nrow),
        "finish",
        [sums, corr, st, z1, z2],
        [],
        out_shape=jax.ShapeDtypeStruct(state.shape, F32),
        out_specs=hbm,
        scratch_shapes=[pltpu.VMEM((lx, kinds, ly), F32), dma((8,))],
    )


def solution(mesh):
    return jax.shard_map(
        functools.partial(body, mesh.shape["gx"], mesh.shape["gy"]),
        mesh=mesh,
        in_specs=(P("gx", None, None, "gy"), P("gx", None, "gy")),
        out_specs=P("gx", None, None, "gy"),
        check_vma=False,
    )
```
